256 devices in a mesh: dp: 32 (over y, x, core), tensor: 8 (over z).
Axes of the slice: x: 4, y: 4, z: 8, core: 2. Of those that a mesh axis runs over, the one named last changes fastest.
Arguments:
- tokens: bfloat16 [24576, 8192], P('dp', 'tensor'), may hold values from -6 to 6
- frozen_weight: bfloat16 [8192, 2048], P('tensor'), may hold values from -0.0625 to 0.0625
- cotangent: bfloat16 [24576, 2048], P('dp', 'tensor'), may hold values from -1.5 to 1.5
- adapter_down_maps: bfloat16 [64, 8192, 64], P('dp', 'tensor'), may hold values from -0.0625 to 0.0625
- adapter_up_maps: bfloat16 [64, 64, 2048], P('dp', None, 'tensor'), may hold values from -0.75 to 0.75
- tenant_stored_row: int32 [64], replicated, may hold values from 0 to 63, as said below
- tenant_per_block: int32 [192], P('dp'), may hold values from 0 to 63, as said below
- block_padding_rows: int32 [192], P('dp'), may hold values from 0 to 64
Outputs:
- kv_out: bfloat16 [24576, 2048], P('dp', 'tensor')
- grad_tokens: bfloat16 [24576, 8192], P('dp', 'tensor')
- grad_down: bfloat16 [64, 8192, 64], P('dp', 'tensor')
- grad_up: bfloat16 [64, 64, 2048], P('dp', None, 'tensor')
The draws below stay inside these ranges and needn't reach their ends.
Inputs may be any that keep to these rules, and one draw needn't show every extreme that they name: A permutation: tenant t's adapters are row tenant_stored_row[t] of adapter_down_maps and adapter_up_maps. `tenant_per_block`: the 6 blocks of one dp index name tenants t whose values tenant_stored_row[t] // 2 are 6 different dp indices.
All inputs are finite; a program needn't handle non-finite values.
Results may differ from the reference program's by a relative error of at most 0.023.
Values may be sent and summed in bfloat16 or wider, within the bound.
A program may use at most 128 MiB of HBM per device.

```python
import jax
import jax.numpy as jnp
from jax import lax

MODEL_WIDTH = 8192
ADAPTER_RANK = 64
BLOCK = 128
TEN_DEV = 2
NBLK = 6
KEY_VALUE_COLS = 2048
TOKENS = 24576
TENANT_TOTAL = 64
N_DP = 32
N_TENSOR = 8


def tenant_plan(key):
    perm_key, heat_key, score_key, slot_key = jax.random.split(key, 4)
    tenant_stored_row = jax.random.permutation(perm_key, TENANT_TOTAL).astype(jnp.int32)
    hotness = jax.random.randint(heat_key, (N_DP,), 0, 4 * N_DP)
    scores = jax.random.randint(score_key, (N_DP, N_DP), 0, 2 * N_DP) + hotness[None, :]
    scores = scores * N_DP + jnp.arange(N_DP, dtype=jnp.int32)[None, :]
    unused_values, owners = lax.top_k(scores, NBLK)
    choices_made = jax.random.randint(slot_key, (N_DP, NBLK, 2), 0, TEN_DEV)
    local_slot = jnp.min(choices_made, axis=2)
    stored = owners.astype(jnp.int32) * TEN_DEV + local_slot
    inverse = jnp.argsort(tenant_stored_row, stable=True).astype(jnp.int32)
    return (tenant_stored_row, jnp.take(inverse, stored.reshape(-1)).astype(jnp.int32))


def draw_tenant_stored_row(key, part):
    return tenant_plan(key)[0]


def draw_tenant_per_block(key, part):
    return tenant_plan(key)[1]


def touch_ends(drawn, rng, smallest, high):
    extent = drawn.shape
    place = [jax.random.randint(jax.random.fold_in(rng, axis), (), 0, extent[axis]) for axis in range(len(extent))]
    drawn = drawn.at[tuple(place)].set(smallest)
    longest = extent.index(max(extent))
    place[longest] = (place[longest] + 1) % extent[longest]
    return drawn.at[tuple(place)].set(high)


def block_levels(key, dims, shards, smallest, high):
    def one(dim, blocks):
        heights = jax.random.uniform(jax.random.fold_in(jax.random.fold_in(key, 6), dim), (blocks,), jnp.float32, smallest / len(shards), high / len(shards))
        return jnp.repeat(jnp.exp(heights), dims[dim] // blocks).reshape((-1,) + (1,) * (len(dims) - dim - 1))

    loudness = one(*shards[0])
    for cut in shards[1:]:
        loudness = loudness * one(*cut)
    return loudness


def noise(rng, shape, deviation, reach, cuts=(), held_as=jnp.bfloat16):
    entries = jax.random.normal(rng, shape, jnp.float32) * deviation
    if len(cuts) > 0:
        entries = block_levels(rng, shape, cuts, -0.22, 0.18) * entries
    return jnp.clip(entries, min=-reach, max=reach).astype(held_as)


def setup_inputs(seed: int = 0) -> dict:
    key_of = jax.random.split(jax.random.key(seed), 9)
    return {
        "tokens": noise(key_of[0], (TOKENS, MODEL_WIDTH), 1.0, 6.0, ((0, 32), (1, 8))),
        "frozen_weight": noise(key_of[1], (MODEL_WIDTH, KEY_VALUE_COLS), MODEL_WIDTH ** -0.5, 0.0625, ((0, 8),)),
        "cotangent": noise(key_of[2], (TOKENS, KEY_VALUE_COLS), 0.25, 1.5, ((0, 32), (1, 8))),
        "adapter_down_maps": noise(key_of[3], (TENANT_TOTAL, MODEL_WIDTH, ADAPTER_RANK), MODEL_WIDTH ** -0.5, 0.0625, ((0, 32), (1, 8))),
        "adapter_up_maps": noise(key_of[4], (TENANT_TOTAL, ADAPTER_RANK, KEY_VALUE_COLS), ADAPTER_RANK ** -0.5, 0.75, ((0, 32), (2, 8))),
        "tenant_stored_row": draw_tenant_stored_row(jax.random.fold_in(key_of[8], 71), 0),
        "tenant_per_block": draw_tenant_per_block(jax.random.fold_in(key_of[8], 71), 0),
        "block_padding_rows": touch_ends(jax.random.randint(key_of[7], (TOKENS // BLOCK,), 0, BLOCK // 2 + 1), jax.random.fold_in(key_of[7], 1), 0, (BLOCK // 2 + 1) - 1).astype(jnp.int32),
    }


def reference(tokens, frozen_weight, cotangent, adapter_down_maps, adapter_up_maps, tenant_stored_row, tenant_per_block, block_padding_rows):
    group_width = MODEL_WIDTH // N_TENSOR
    base_out = jnp.zeros((TOKENS, KEY_VALUE_COLS), jnp.float32)
    for group_index in range(N_TENSOR):
        lower = group_index * group_width
        partial_out = jnp.dot(tokens[:, lower:lower + group_width], frozen_weight[lower:lower + group_width], preferred_element_type=jnp.float32)
        rounded = lax.optimization_barrier(partial_out.astype(jnp.bfloat16))
        base_out = base_out + rounded.astype(jnp.float32)
    storage_position = jnp.take(tenant_stored_row, tenant_per_block).astype(jnp.int32)
    position = jnp.arange(BLOCK, dtype=jnp.int32)
    weight_t = frozen_weight.T

    def one_block(current_block):
        row_start = (current_block * BLOCK).astype(jnp.int32)
        row_block = lax.dynamic_slice_in_dim(tokens, row_start, BLOCK, 0)
        base_rows = lax.dynamic_slice_in_dim(base_out, row_start, BLOCK, 0)
        cot_rows = lax.dynamic_slice_in_dim(cotangent, row_start, BLOCK, 0)
        down_weight_slab = adapter_down_maps[storage_position[current_block]]
        up_weight_slab = adapter_up_maps[storage_position[current_block]]
        live_rows = (position < BLOCK - block_padding_rows[current_block]).astype(jnp.float32)[:, None]
        low_rank = jnp.dot(row_block, down_weight_slab, preferred_element_type=jnp.float32).astype(jnp.bfloat16)
        low_lift = jnp.dot(low_rank, up_weight_slab, preferred_element_type=jnp.float32)
        out_rows = (live_rows * (base_rows + 0.5 * low_lift)).astype(jnp.bfloat16)
        grad_rows = (cot_rows.astype(jnp.float32) * live_rows).astype(jnp.bfloat16)
        back_low = (0.5 * jnp.dot(grad_rows, up_weight_slab.T, preferred_element_type=jnp.float32)).astype(jnp.bfloat16)
        token_grad = jnp.dot(grad_rows, weight_t, preferred_element_type=jnp.float32) + jnp.dot(back_low, down_weight_slab.T, preferred_element_type=jnp.float32)
        down_term = jnp.dot(row_block.T, back_low, preferred_element_type=jnp.float32).astype(jnp.bfloat16)
        up_term = (0.5 * jnp.dot(low_rank.T, grad_rows, preferred_element_type=jnp.float32)).astype(jnp.bfloat16)
        return out_rows, token_grad.astype(jnp.bfloat16), down_term, up_term

    block_count = TOKENS // BLOCK
    kv_blocks, grad_blocks, down_terms, up_terms = lax.map(one_block, jnp.arange(block_count, dtype=jnp.int32))
    kv_out = kv_blocks.reshape(TOKENS, KEY_VALUE_COLS)
    grad_tokens = grad_blocks.reshape(TOKENS, MODEL_WIDTH)
    grad_down = jnp.zeros((TENANT_TOTAL, MODEL_WIDTH, ADAPTER_RANK), jnp.float32).at[storage_position].add(down_terms.astype(jnp.float32)).astype(jnp.bfloat16)
    grad_up = jnp.zeros((TENANT_TOTAL, ADAPTER_RANK, KEY_VALUE_COLS), jnp.float32).at[storage_position].add(up_terms.astype(jnp.float32)).astype(jnp.bfloat16)
    return kv_out, grad_tokens, grad_down, grad_up
```

```python
import jax
import jax.numpy as jnp
from jax import lax
from jax.experimental import pallas as pl
from jax.experimental.pallas import tpu as pltpu
from jax.sharding import PartitionSpec as P

MESH = pl.DeviceIdType.MESH
F32, BF16, I32 = jnp.float32, jnp.bfloat16, jnp.int32
NT = (((1,), (1,)), ((), ()))
TN = (((0,), (0,)), ((), ()))
NZ, NB, BR = 8, 6, 128
ROWS, HALF = 768, 384
FEAT, COLS, RANK, HR = 1024, 256, 64, 32
N_SEM = 160


def mm(a, b, dims=None):
    if dims is None:
        return jnp.dot(a, b, preferred_element_type=F32)
    return lax.dot_general(a, b, dims, preferred_element_type=F32)


def kernel(
    stored, tenants, padding, tok_in, w_in, cot_in, down_in, up_in,
    kv_out, gt_out, gd_out, gu_out,
    tok, w, g, acc, rs_right, rs_left, rs_first, kv, gt,
    ad, au, dsel, usel, dsib, usib, ints, ints_smem, table,
    low_part, low_recv, low, back_part, back_recv, back,
    td, tu, rd, ru, qd, qu, qd_in, qu_in, fd, fu, fd_in, fu_in,
    send_sem, recv_sem, load_sem, store_sem, copy_sem,
):
    dp, z = lax.axis_index("dp"), lax.axis_index("tensor")
    y, x, c = dp // 8, (dp // 2) % 4, dp % 2
    mp, mq = (1 - c) * x + c * y, (1 - c) * y + c * x

    def z_at(step):
        return (dp, (z + step + NZ) % NZ)

    def p_at(step):
        return (((y + c * step + 4) % 4) * 8 + ((x + (1 - c) * step + 4) % 4) * 2 + c, z)

    def q_at(step):
        return (((y + (1 - c) * step + 4) % 4) * 8 + ((x + c * step + 4) % 4) * 2 + c, z)

    sibling = (dp + 1 - 2 * c, z)
    sent = {}

    def send(key, src, dst, device):
        n = len(sent)
        copy = pltpu.make_async_remote_copy(
            src_ref=src, dst_ref=dst, send_sem=send_sem.at[n], recv_sem=recv_sem.at[n],
            device_id=device, device_id_type=MESH,
        )
        copy.start()
        sent[key] = copy

    def recv(key):
        sent[key].wait_recv()

    loads = {}

    def load(key, src, dst):
        loads[key] = pltpu.make_async_copy(src, dst, load_sem.at[len(loads)])
        loads[key].start()

    load("g", cot_in, g.at[0])
    load("u", up_in.at[:, pl.ds(c * HR, HR)], au.at[0, 0, pl.ds(2 * c, 2)])
    load("d", down_in.at[:, pl.ds(c * HR, HR)], ad.at[0, 0, pl.ds(2 * c, 2)])
    load("tok", tok_in, tok)

    def load_w(k):
        load(("w", k), w_in.at[:, pl.ds(((z + k) % NZ) * COLS, COLS)], w.at[k])

    for k in (4, 3, 5, 0, 2, 6, 1, 7):
        load_w(k)

    barrier = pltpu.get_barrier_semaphore()
    friends = [z_at(k) for k in range(1, NZ)] + [p_at(1), p_at(-1), q_at(1), q_at(-1), sibling]
    for friend in friends:
        pl.semaphore_signal(barrier, inc=1, device_id=friend, device_id_type=MESH)

    lane = lax.broadcasted_iota(I32, (8, 128), 1)
    mine = jnp.zeros((8, 128), I32)
    for b in range(NB):
        mine = jnp.where(lane == b, stored[tenants[b]], mine)
    ints[0, c] = mine

    loads["g"].wait()
    position = lax.broadcasted_iota(I32, (BR, 1), 0)

    def live(b):
        return (position < BR - padding[b]).astype(F32)

    for b in range(NB):
        rows = pl.ds(b * BR, BR)
        g[0, rows] = (g[0, rows].astype(F32) * live(b)).astype(BF16)

    pl.semaphore_wait(barrier, len(friends))

    half = (pl.ds(0, HALF), pl.ds(HALF, HALF))

    def ag_send(step, h, right):
        src, dst = ((-step) % NZ, (-step - 1) % NZ) if right else (step, step + 1)
        send(("ag", right, step, h), g.at[src, half[h]], g.at[dst, half[h]], z_at(1 if right else -1))

    def ag_pass(step, h, right):
        recv(("ag", right, step, h))
        ag_send(step + 1, h, right)

    for h in (0, 1):
        ag_send(0, h, True)
        ag_send(0, h, False)

    send("f0i", ints.at[0, c], ints.at[0, c], sibling)
    send("f0u", up_in.at[:, pl.ds((1 - c) * HR, HR)], au.at[0, 0, pl.ds(2 * c, 2)], sibling)
    send("f0d", down_in.at[:, pl.ds((1 - c) * HR, HR)], ad.at[0, 0, pl.ds(2 * c, 2)], sibling)

    def partial(k, h):
        return mm(tok[half[h]], w[k])

    def rs_start(step, h, right):
        k = (4 - step) if right else (4 + step)
        slot = step * 2 + (0 if right else 1)
        rs_first[slot] = partial(k, h).astype(BF16)
        dst = rs_right if right else rs_left
        send(("rs", right, step, h), rs_first.at[slot], dst.at[step, half[h]], z_at(1 if right else -1))

    def rs_pass(step, h, right):
        k = (4 - step) if right else (4 + step)
        buf = rs_right if right else rs_left
        own = partial(k, h)
        recv(("rs", right, step - 1, h))
        buf[step - 1, half[h]] = (buf[step - 1, half[h]].astype(F32) + own).astype(BF16)
        send(("rs", right, step, h), buf.at[step - 1, half[h]], buf.at[step, half[h]], z_at(1 if right else -1))

    loads["tok"].wait()
    loads[("w", 4)].wait()
    rs_start(0, 0, True)
    rs_start(0, 1, False)
    loads[("w", 3)].wait()
    rs_start(1, 1, True)
    loads[("w", 5)].wait()
    rs_start(1, 0, False)

    def f1_send(name, a):
        send((name, "f1", 1), a.at[0, 0], a.at[0, 3], p_at(1))
        send((name, "f1", -1), a.at[0, 0], a.at[0, 1], p_at(-1))

    def f1_pass(name, a):
        recv((name, "f1", 1))
        send((name, "f1x", 1), a.at[0, 3, pl.ds(0, 2)], a.at[0, 2, pl.ds(0, 2)], p_at(1))
        recv((name, "f1", -1))
        send((name, "f1x", -1), a.at[0, 1, pl.ds(2, 2)], a.at[0, 2, pl.ds(2, 2)], p_at(-1))

    def f1_end(name):
        recv((name, "f1x", 1))
        recv((name, "f1x", -1))

    def f2_send(name, a, rp):
        send((name, "f2", 1, rp), a.at[0, rp], a.at[3, rp], q_at(1))
        send((name, "f2", -1, rp), a.at[0, rp], a.at[1, rp], q_at(-1))

    def f2_pass(name, a, rp):
        recv((name, "f2", 1, rp))
        send((name, "f2x", 1, rp), a.at[3, rp, pl.ds(0, 2)], a.at[2, rp, pl.ds(0, 2)], q_at(1))
        recv((name, "f2", -1, rp))
        send((name, "f2x", -1, rp), a.at[1, rp, pl.ds(2, 2)], a.at[2, rp, pl.ds(2, 2)], q_at(-1))

    def f2_end(name):
        for rp in range(4):
            recv((name, "f2x", 1, rp))
            recv((name, "f2x", -1, rp))

    loads["u"].wait()
    recv("f0u")
    f1_send("u", au)
    f2_send("u", au, 0)
    recv("f0i")
    send(("i", 1), ints.at[0], ints.at[3], q_at(1))
    send(("i", -1), ints.at[0], ints.at[1], q_at(-1))
    loads["d"].wait()
    recv("f0d")
    f1_send("d", ad)
    f2_send("d", ad, 0)
    f1_pass("u", au)
    f2_send("u", au, 3)
    f2_send("u", au, 1)
    recv(("i", 1))
    send(("i", 2), ints.at[3], ints.at[2], q_at(1))
    recv(("i", -1))
    f1_end("u")
    f2_send("u", au, 2)
    f2_pass("u", au, 0)
    f1_pass("d", ad)
    f2_send("d", ad, 3)
    f2_send("d", ad, 1)

    def acc_first():
        def body(i, _):
            rows = pl.ds(i * 256, 256)
            acc[rows] = mm(g[0, rows], w[0], NT)
            return 0

        lax.fori_loop(0, 3, body, 0)

    def acc_pair(k):
        def body(i, _):
            rows = pl.ds(i * 256, 256)
            acc[rows] += mm(g[k, rows], w[k], NT) + mm(g[NZ - k, rows], w[NZ - k], NT)
            return 0

        lax.fori_loop(0, 3, body, 0)

    loads[("w", 0)].wait()
    acc_first()
    f2_pass("u", au, 3)
    f2_pass("u", au, 1)
    f2_pass("u", au, 2)
    recv(("i", 2))
    to_smem = pltpu.make_async_copy(ints, ints_smem, copy_sem.at[0])
    to_smem.start()
    to_smem.wait()

    def place(slot):
        chip, inner = slot // 4, slot % 4
        cy, cx = chip // 4, chip % 4
        rq = ((1 - c) * cy + c * cx - mq + 4) % 4
        rp = ((1 - c) * cx + c * cy - mp + 4) % 4
        return rq, rp, inner

    def pick(name, a, sel, sib):
        for b in range(NB):
            rq, rp, inner = place(ints_smem[0, 1 - c, 0, b])
            sib[b] = a[rq, rp, inner]
        send((name, "sib"), sib, sel.at[c], sibling)
        for b in range(NB):
            rq, rp, inner = place(ints_smem[0, c, 0, b])
            sel[c, b] = a[rq, rp, inner]

    def panel(sel, b):
        return jnp.concatenate([sel[0, b], sel[1, b]], axis=0)

    def sum_scatter(name, part, got):
        for k in range(1, NZ):
            rows = pl.ds(((z + k) % NZ) * 48, 48)
            send((name, "s", k), part.at[rows], got.at[k], z_at(k))

    def sum_gather(name, part, got, total, scale):
        own = pl.ds(z * 48, 48)
        value = part[own].astype(F32)
        for k in range(1, NZ):
            recv((name, "s", k))
            value = value + got[k].astype(F32)
        total[own] = (value * scale).astype(BF16)
        for k in range(1, NZ):
            send((name, "g", k), total.at[own], total.at[own], z_at(k))

    def sum_end(name):
        for k in range(1, NZ):
            recv((name, "g", k))

    for h in (0, 1):
        ag_pass(0, h, True)
        ag_pass(0, h, False)
    f2_end("u")
    pick("u", au, usel, usib)
    recv(("u", "sib"))
    for b in range(NB):
        back_part[pl.ds(b * RANK, RANK)] = mm(panel(usel, b), g[0, pl.ds(b * BR, BR)], NT).astype(BF16)
    sum_scatter("back", back_part, back_recv)
    loads[("w", 2)].wait()
    loads[("w", 6)].wait()
    loads[("w", 1)].wait()
    loads[("w", 7)].wait()
    f1_end("d")
    f2_send("d", ad, 2)
    f2_pass("d", ad, 0)
    rs_pass(1, 0, True)
    rs_pass(1, 1, False)
    f2_pass("d", ad, 3)
    f2_pass("d", ad, 1)
    sum_gather("back", back_part, back_recv, back, 0.5)
    acc_pair(1)

    def fill_table(j, _):
        pj = (mp + j // 4) % 4
        slot = (((1 - c) * mq + c * pj) * 4 + (1 - c) * pj + c * mq) * 4 + j % 4
        for i in range(4):
            for core in range(2):
                entry = I32(48)
                for b in range(NB):
                    entry = jnp.where(ints_smem[i, core, 0, b] == slot, (i * 2 + core) * NB + b, entry)
                table[j, i * 2 + core] = entry
        return 0

    lax.fori_loop(0, 16, fill_table, 0)
    rd[48] = jnp.zeros((HR, FEAT), BF16)
    ru[48] = jnp.zeros((HR, COLS), BF16)

    for h in (0, 1):
        ag_pass(1, h, True)
        ag_pass(1, h, False)
    for h in (0, 1):
        rs_pass(2, h, True)
        rs_pass(2, h, False)

    def terms_out(name, t, r, sem):
        send((name, "t0"), t.at[1 - c], r.at[pl.ds(c * NB, NB)], sibling)
        send((name, "t1", 1), t.at[c], r.at[pl.ds(36 + c * NB, NB)], q_at(1))
        send((name, "t1", -1), t.at[c], r.at[pl.ds(12 + c * NB, NB)], q_at(-1))
        own = pltpu.make_async_copy(t.at[c], r.at[pl.ds(c * NB, NB)], copy_sem.at[sem])
        own.start()
        return own

    def terms_sibling(name, t, r):
        recv((name, "t0"))
        other = (1 - c) * NB
        send((name, "t2", 1), r.at[pl.ds(other, NB)], r.at[pl.ds(36 + other, NB)], q_at(1))
        send((name, "t2", -1), r.at[pl.ds(other, NB)], r.at[pl.ds(12 + other, NB)], q_at(-1))

    def terms_pass(name, t, r):
        recv((name, "t1", 1))
        recv((name, "t2", 1))
        send((name, "t3", 1), r.at[pl.ds(36, NB)], r.at[pl.ds(24, NB)], q_at(1))
        recv((name, "t1", -1))
        recv((name, "t2", -1))
        send((name, "t3", -1), r.at[pl.ds(12 + NB, NB)], r.at[pl.ds(24 + NB, NB)], q_at(-1))

    def add_up(r, q, j):
        def body(inner, _):
            total = r[table[j * 4 + inner, 0]].astype(F32)
            for d in range(1, 8):
                total = total + r[table[j * 4 + inner, d]].astype(F32)
            q[j, inner] = total.astype(BF16)
            return 0

        lax.fori_loop(0, 4, body, 0)

    def sums_out(name, r, q, q_in):
        recv((name, "t3", 1))
        recv((name, "t3", -1))
        add_up(r, q, 2)
        send((name, "q0", 1), q.at[2, pl.ds(0, 2)], q_in.at[0, pl.ds(0, 2)], p_at(1))
        send((name, "q0", -1), q.at[2, pl.ds(2, 2)], q_in.at[0, pl.ds(2, 2)], p_at(-1))
        add_up(r, q, 1)
        add_up(r, q, 3)
        add_up(r, q, 0)

    def sums_pass(name, q, q_in):
        recv((name, "q0", 1))
        q[1, 0:2] = (q[1, 0:2].astype(F32) + q_in[0, 0:2].astype(F32)).astype(BF16)
        send((name, "q1", 1), q.at[1], q_in.at[1], p_at(1))
        recv((name, "q0", -1))
        q[3, 2:4] = (q[3, 2:4].astype(F32) + q_in[0, 2:4].astype(F32)).astype(BF16)
        send((name, "q1", -1), q.at[3], q_in.at[2], p_at(-1))

    def sums_end(name, q, q_in, f, f_in):
        recv((name, "q1", 1))
        recv((name, "q1", -1))
        for k in range(4):
            f[k] = (q[0, k].astype(F32) + q_in[1, k].astype(F32) + q_in[2, k].astype(F32)).astype(BF16)
        send((name, "t9"), f.at[pl.ds(2 - 2 * c, 2)], f_in, sibling)

    stores = []

    def store(src, dst):
        stores.append(pltpu.make_async_copy(src, dst, store_sem.at[len(stores)]))
        stores[-1].start()

    def sums_store(name, f, f_in, out):
        store(f.at[pl.ds(2 * c, 2)], out.at[:, pl.ds(c * HR, HR)])
        recv((name, "t9"))
        store(f_in, out.at[:, pl.ds((1 - c) * HR, HR)])

    sum_end("back")
    for b in range(NB):
        term = mm(back[pl.ds(b * RANK, RANK)], tok[pl.ds(b * BR, BR)]).astype(BF16)
        td[0, b] = term[:HR]
        td[1, b] = term[HR:]
    own_d = terms_out("d", td, rd, 1)
    f2_pass("d", ad, 2)
    f2_end("d")
    pick("d", ad, dsel, dsib)
    terms_sibling("d", td, rd)
    recv(("d", "sib"))
    for b in range(NB):
        low_part[pl.ds(b * RANK, RANK)] = mm(panel(dsel, b), tok[pl.ds(b * BR, BR)], NT).astype(BF16)
    sum_scatter("low", low_part, low_recv)
    acc_pair(2)
    ag_pass(2, 0, True)
    ag_pass(2, 1, False)
    sum_gather("low", low_part, low_recv, low, 1.0)
    for h in (0, 1):
        rs_pass(3, h, True)
        rs_pass(3, h, False)
    terms_pass("d", td, rd)
    for b in range(NB):
        rows = pl.ds(b * BR, BR)
        acc[rows] += mm(back[pl.ds(b * RANK, RANK)], panel(dsel, b), TN)
    sum_end("low")
    for b in range(NB):
        term = (0.5 * mm(low[pl.ds(b * RANK, RANK)], g[0, pl.ds(b * BR, BR)])).astype(BF16)
        tu[0, b] = term[:HR]
        tu[1, b] = term[HR:]
    own_u = terms_out("u", tu, ru, 2)
    own_d.wait()
    own_u.wait()
    terms_sibling("u", tu, ru)
    sums_out("d", rd, qd, qd_in)
    terms_pass("u", tu, ru)
    sums_pass("d", qd, qd_in)
    recv(("ag", True, 2, 1))
    recv(("ag", False, 2, 0))
    acc_pair(3)
    sums_out("u", ru, qu, qu_in)
    sums_end("d", qd, qd_in, fd, fd_in)
    sums_pass("u", qu, qu_in)
    sums_store("d", fd, fd_in, gd_out)
    sums_end("u", qu, qu_in, fu, fu_in)

    recv(("ag", True, 3, 0))
    recv(("ag", False, 3, 1))

    def last_rows(i, _):
        rows = pl.ds(i * 256, 256)
        gt[rows] = (acc[rows] + mm(g[4, rows], w[4], NT)).astype(BF16)
        return 0

    lax.fori_loop(0, 3, last_rows, 0)
    store(gt, gt_out)
    sums_store("u", fu, fu_in, gu_out)

    for h in (0, 1):
        base = partial(0, h)
        recv(("rs", True, 3, h))
        recv(("rs", False, 3, h))
        for i in range(3):
            b = h * 3 + i
            rows = pl.ds(b * BR, BR)
            lift = mm(low[pl.ds(b * RANK, RANK)], panel(usel, b), TN)
            base_rows = base[i * BR : (i + 1) * BR] + rs_right[3, rows].astype(F32) + rs_left[3, rows].astype(F32)
            kv[rows] = (live(b) * (base_rows + 0.5 * lift)).astype(BF16)
        store(kv.at[half[h]], kv_out.at[half[h]])

    for copy in sent.values():
        copy.wait_send()
    for copy in stores:
        copy.wait()


def local(tokens, frozen_weight, cotangent, down_maps, up_maps, stored_row, tenants, padding):
    shape = jax.ShapeDtypeStruct
    smem, anywhere = pl.BlockSpec(memory_space=pltpu.SMEM), pl.BlockSpec(memory_space=pl.ANY)
    vmem = pltpu.VMEM
    kv, gt, gd, gu = pl.pallas_call(
        kernel,
        name="projections",
        out_shape=(
            shape((ROWS, COLS), BF16), shape((ROWS, FEAT), BF16),
            shape((2, RANK, FEAT), BF16), shape((2, RANK, COLS), BF16),
        ),
        in_specs=[smem] * 3 + [anywhere] * 5,
        out_specs=[anywhere] * 4,
        scratch_shapes=[
            vmem((ROWS, FEAT), BF16),
            vmem((NZ, FEAT, COLS), BF16),
            vmem((NZ, ROWS, COLS), BF16),
            vmem((ROWS, FEAT), F32),
            vmem((4, ROWS, COLS), BF16),
            vmem((4, ROWS, COLS), BF16),
            vmem((4, HALF, COLS), BF16),
            vmem((ROWS, COLS), BF16),
            vmem((ROWS, FEAT), BF16),
            vmem((4, 4, 4, HR, FEAT), BF16),
            vmem((4, 4, 4, HR, COLS), BF16),
            vmem((2, NB, HR, FEAT), BF16),
            vmem((2, NB, HR, COLS), BF16),
            vmem((NB, HR, FEAT), BF16),
            vmem((NB, HR, COLS), BF16),
            vmem((4, 2, 8, 128), I32),
            pltpu.SMEM((4, 2, 8, 128), I32),
            pltpu.SMEM((16, 8), I32),
            vmem((NB * RANK, BR), BF16),
            vmem((NZ, 48, BR), BF16),
            vmem((NB * RANK, BR), BF16),
            vmem((NB * RANK, BR), BF16),
            vmem((NZ, 48, BR), BF16),
            vmem((NB * RANK, BR), BF16),
            vmem((2, NB, HR, FEAT), BF16),
            vmem((2, NB, HR, COLS), BF16),
            vmem((49, HR, FEAT), BF16),
            vmem((49, HR, COLS), BF16),
            vmem((4, 4, HR, FEAT), BF16),
            vmem((4, 4, HR, COLS), BF16),
            vmem((3, 4, HR, FEAT), BF16),
            vmem((3, 4, HR, COLS), BF16),
            vmem((4, HR, FEAT), BF16),
            vmem((4, HR, COLS), BF16),
            vmem((2, HR, FEAT), BF16),
            vmem((2, HR, COLS), BF16),
            pltpu.SemaphoreType.DMA((N_SEM,)),
            pltpu.SemaphoreType.DMA((N_SEM,)),
            pltpu.SemaphoreType.DMA((16,)),
            pltpu.SemaphoreType.DMA((8,)),
            pltpu.SemaphoreType.DMA((4,)),
        ],
        compiler_params=pltpu.CompilerParams(
            collective_id=0, has_side_effects=True, vmem_limit_bytes=56 * 2**20
        ),
    )(
        stored_row, tenants, padding, tokens, frozen_weight, cotangent,
        jnp.swapaxes(down_maps, 1, 2), up_maps,
    )
    return kv, gt, jnp.swapaxes(gd, 1, 2), gu


def solution(mesh):
    placed = (
        P("dp", "tensor"),
        P("tensor", None),
        P("dp", "tensor"),
        P("dp", "tensor", None),
        P("dp", None, "tensor"),
        P(),
        P("dp"),
        P("dp"),
    )
    return jax.shard_map(
        local,
        mesh=mesh,
        in_specs=placed,
        out_specs=(
            P("dp", "tensor"),
            P("dp", "tensor"),
            P("dp", "tensor", None),
            P("dp", None, "tensor"),
        ),
        check_vma=False,
    )
```

```python
import jax
import jax.numpy as jnp
from jax import lax
from jax.experimental import pallas as pl
from jax.experimental.pallas import tpu as pltpu
from jax.sharding import PartitionSpec as P

MESH = pl.DeviceIdType.MESH
F32, BF16, I32 = jnp.float32, jnp.bfloat16, jnp.int32
NT = (((1,), (1,)), ((), ()))
TN = (((0,), (0,)), ((), ()))
NZ, NB, BR = 8, 6, 128
ROWS, HALF = 768, 384
FEAT, COLS, RANK, HR = 1024, 256, 64, 32
N_SEM = 160


def mm(a, b, dims=None):
    if dims is None:
        return jnp.dot(a, b, preferred_element_type=F32)
    return lax.dot_general(a, b, dims, preferred_element_type=F32)


def kernel(
    stored, tenants, padding, tok_in, w_in, cot_in, down_in, up_in,
    kv, gt, gd, gu,
    tok, w, g, g_sib, acc, kv_acc, rs_right, rs_left, rs_first,
    ad, au, dh, uh, dx, ux, ints, ints_smem, table,
    low_part, low_recv, low, low_x, back_part, back_recv, back, back_x,
    rd, ru, qd, qu, qd_in, qu_in,
    send_sem, recv_sem, load_sem, copy_sem,
):
    dp, z = lax.axis_index("dp"), lax.axis_index("tensor")
    y, x, c = dp // 8, (dp // 2) % 4, dp % 2
    mp, mq = (1 - c) * x + c * y, (1 - c) * y + c * x

    def z_at(step):
        return (dp, (z + step + NZ) % NZ)

    def chip_at(dy, dx_, core):
        return (((y + dy + 4) % 4) * 8 + ((x + dx_ + 4) % 4) * 2 + core, z)

    def p_at(step):
        return chip_at(c * step, (1 - c) * step, c)

    def q_at(step):
        return chip_at((1 - c) * step, c * step, c)

    def p_cross(step):
        return chip_at(c * step, (1 - c) * step, 1 - c)

    def q_cross(step):
        return chip_at((1 - c) * step, c * step, 1 - c)

    sibling = (dp + 1 - 2 * c, z)
    sent = {}

    def send(key, src, dst, device):
        n = len(sent)
        copy = pltpu.make_async_remote_copy(
            src_ref=src, dst_ref=dst, send_sem=send_sem.at[n], recv_sem=recv_sem.at[n],
            device_id=device, device_id_type=MESH,
        )
        copy.start()
        sent[key] = copy

    arrived = set()

    def recv(key):
        if key not in arrived:
            arrived.add(key)
            sent[key].wait_recv()

    loads = {}

    def load(key, src, dst):
        loads[key] = pltpu.make_async_copy(src, dst, load_sem.at[len(loads)])
        loads[key].start()

    mine, others = pl.ds(c * HR, HR), pl.ds((1 - c) * HR, HR)
    load("g", cot_in, g.at[0])
    load("u", up_in.at[:, mine], au.at[0, 0, 0])
    load("d", down_in.at[:, mine], ad.at[0, 0, 0])
    load("tok", tok_in, tok.at[0])
    for k in (4, 3, 5, 0, 2, 6, 1, 7):
        load(("w", k), w_in.at[:, pl.ds(((z + k) % NZ) * COLS, COLS)], w.at[k])

    barrier = pltpu.get_barrier_semaphore()
    friends = [z_at(k) for k in range(1, NZ)] + [p_at(1), p_at(-1), q_at(1), q_at(-1), sibling]
    friends += [q_cross(1), q_cross(-1)]
    for friend in friends:
        pl.semaphore_signal(barrier, inc=1, device_id=friend, device_id_type=MESH)

    lane = lax.broadcasted_iota(I32, (8, 128), 1)
    tile = jnp.zeros((8, 128), I32)
    for b in range(NB):
        tile = jnp.where(lane == b, stored[tenants[b]], tile)
    ints[0, 0] = tile

    position = lax.broadcasted_iota(I32, (BR, 1), 0)

    def live(b):
        return (position < BR - padding[b]).astype(F32)

    loads["g"].wait()
    for b in range(NB):
        rows = pl.ds(b * BR, BR)
        g[0, rows] = (g[0, rows].astype(F32) * live(b)).astype(BF16)

    pl.semaphore_wait(barrier, len(friends))

    half = (pl.ds(0, HALF), pl.ds(HALF, HALF))

    def ag_send(step, h, right):
        src, dst = ((-step) % NZ, (-step - 1) % NZ) if right else (step, step + 1)
        send(("ag", right, step, h), g.at[src, half[h]], g.at[dst, half[h]], z_at(1 if right else -1))

    def ag_pass(step, h):
        for right in (True, False):
            recv(("ag", right, step, h))
            if step < 2 or (h == 0) == right:
                ag_send(step + 1, h, right)

    def partial(k, h):
        return mm(tok[0, half[h]], w[k])

    def rs_start(step, h, right):
        k = (4 - step) if right else (4 + step)
        slot = step * 2 + (0 if right else 1)
        rs_first[slot] = partial(k, h).astype(BF16)
        dst = rs_right if right else rs_left
        send(("rs", right, step, h), rs_first.at[slot], dst.at[step, half[h]], z_at(1 if right else -1))

    def rs_pass(step, h):
        for right in (True, False):
            if step == 1 and (h == 0) != right:
                continue
            k = (4 - step) if right else (4 + step)
            buf = rs_right if right else rs_left
            own = partial(k, h)
            recv(("rs", right, step - 1, h))
            buf[step - 1, half[h]] = (buf[step - 1, half[h]].astype(F32) + own).astype(BF16)
            send(("rs", right, step, h), buf.at[step - 1, half[h]], buf.at[step, half[h]], z_at(1 if right else -1))

    def f1_send(name, a, r):
        send((name, "f1", 1, r), a.at[0, 0, r], a.at[0, 3, r], p_at(1))
        send((name, "f1", -1, r), a.at[0, 0, r], a.at[0, 1, r], p_at(-1))

    def f1_pass(name, a):
        recv((name, "f1", 1, 0))
        send((name, "f1x", 1), a.at[0, 3, 0], a.at[0, 2, 0], p_at(1))
        recv((name, "f1", -1, 1))
        send((name, "f1x", -1), a.at[0, 1, 1], a.at[0, 2, 1], p_at(-1))
        recv((name, "f1", 1, 1))
        recv((name, "f1", -1, 0))

    def f1_end(name):
        recv((name, "f1x", 1))
        recv((name, "f1x", -1))

    def f2_send(name, a, rp):
        send((name, "f2", 1, rp), a.at[0, rp], a.at[3, rp], q_at(1))
        send((name, "f2", -1, rp), a.at[0, rp], a.at[1, rp], q_at(-1))

    def f2_pass(name, a, rp):
        recv((name, "f2", 1, rp))
        send((name, "f2x", 1, rp), a.at[3, rp, 0], a.at[2, rp, 0], q_at(1))
        recv((name, "f2", -1, rp))
        send((name, "f2x", -1, rp), a.at[1, rp, 1], a.at[2, rp, 1], q_at(-1))

    def f2_end(name):
        for rp in range(4):
            recv((name, "f2x", 1, rp))
            recv((name, "f2x", -1, rp))

    def fetch_0(name, a):
        recv((name, "f0"))
        f1_send(name, a, 1)
        f2_send(name, a, 0)

    def fetch_1(name, a):
        f1_pass(name, a)
        f2_send(name, a, 3)
        f2_send(name, a, 1)

    def fetch_2(name, a):
        f1_end(name)
        f2_send(name, a, 2)

    def fetch_3(name, a):
        f2_pass(name, a, 0)

    def fetch_4(name, a):
        f2_pass(name, a, 3)
        f2_pass(name, a, 1)

    def fetch_5(name, a):
        f2_pass(name, a, 2)

    def place(slot):
        chip, inner = slot // 4, slot % 4
        cy, cx = chip // 4, chip % 4
        rq = ((1 - c) * cy + c * cx - mq + 4) % 4
        rp = ((1 - c) * cx + c * cy - mp + 4) % 4
        return rq, rp, (inner // 2 + c) % 2, inner % 2

    def pick(name, a, picked, out):
        f2_end(name)
        for r in (1, 0):
            for b in range(NB):
                rq, rp, core, inner = place(ints_smem[0, r, 0, b])
                picked[r, b] = a[rq, rp, core, inner]
        send((name, "pick"), picked.at[1], out, sibling)

    def sum_scatter(name, part, got):
        for k in range(1, NZ):
            rows = pl.ds(((z + k) % NZ) * 48, 48)
            send((name, "s", k), part.at[rows], got.at[k], z_at(k))

    def sum_gather(name, part, got, total, scale):
        own = pl.ds(z * 48, 48)
        value = part[own].astype(F32)
        for k in range(1, NZ):
            recv((name, "s", k))
            value = value + got[k].astype(F32)
        total[own] = (value * scale).astype(BF16)
        for k in range(1, NZ):
            send((name, "g", k), total.at[own], total.at[own], z_at(k))

    def sum_end(name, total, out):
        for k in range(1, NZ):
            recv((name, "g", k))
        send((name, "x"), total.at[pl.ds(NB * HR, NB * HR)], out, sibling)

    def rank_rows(r, b):
        return pl.ds((r * NB + b) * HR, HR)

    def block(b):
        return pl.ds(b * BR, BR)

    def back_begin():
        pick("u", au, uh, ux)
        recv("xg")
        for b in range(NB):
            back_part[rank_rows(0, b)] = mm(uh[0, b], g[0, block(b)], NT).astype(BF16)
            back_part[rank_rows(1, b)] = mm(uh[1, b], g_sib[block(b)], NT).astype(BF16)
        sum_scatter("back", back_part, back_recv)

    def low_begin():
        pick("d", ad, dh, dx)
        recv("xtok")
        for r in (0, 1):
            for b in range(NB):
                low_part[rank_rows(r, b)] = mm(dh[r, b], tok[r, block(b)], NT).astype(BF16)
        sum_scatter("low", low_part, low_recv)

    def terms_send(name, r, core):
        src = r.at[pl.ds(core * NB, NB)]
        send((name, "t1", 1, core), src, r.at[pl.ds(36 + core * NB, NB)], q_at(1))
        send((name, "t1", -1, core), src, r.at[pl.ds(12 + core * NB, NB)], q_at(-1))

    def down_terms():
        sum_end("back", back, back_x)
        recv("xtok")
        for r in (0, 1):
            for b in range(NB):
                rd[r * NB + b] = mm(back[rank_rows(r, b)], tok[r, block(b)]).astype(BF16)
            terms_send("d", rd, r)

    def up_terms():
        sum_end("low", low, low_x)
        for b in range(NB):
            ru[b] = (0.5 * mm(low[rank_rows(0, b)], g[0, block(b)])).astype(BF16)
        terms_send("u", ru, 0)
        for b in range(NB):
            ru[NB + b] = (0.5 * mm(low[rank_rows(1, b)], g_sib[block(b)])).astype(BF16)
        terms_send("u", ru, 1)

    def terms_pass(name, r):
        recv((name, "t1", 1, 0))
        send((name, "t2", 1), r.at[pl.ds(36, NB)], r.at[pl.ds(24, NB)], q_at(1))
        recv((name, "t1", -1, 1))
        send((name, "t2", -1), r.at[pl.ds(12 + NB, NB)], r.at[pl.ds(24 + NB, NB)], q_at(-1))
        recv((name, "t1", 1, 1))
        recv((name, "t1", -1, 0))

    def fill_table():
        rd[48] = jnp.zeros((HR, FEAT), BF16)
        ru[48] = jnp.zeros((HR, COLS), BF16)

        def body(j, _):
            pj, core = (mp + j // 4) % 4, (j // 2 + c) % 2
            slot = (((1 - c) * mq + c * pj) * 4 + (1 - c) * pj + c * mq) * 4 + core * 2 + j % 2
            for i in range(4):
                for r in range(2):
                    entry = I32(48)
                    for b in range(NB):
                        entry = jnp.where(ints_smem[i, r, 0, b] == slot, (i * 2 + r) * NB + b, entry)
                    table[j, i * 2 + r] = entry
            return 0

        lax.fori_loop(0, 16, body, 0)

    def add_up(r, q, j):
        def body(inner, _):
            total = r[table[j * 4 + inner, 0]].astype(F32)
            for d in range(1, 8):
                total = total + r[table[j * 4 + inner, d]].astype(F32)
            q[j, inner // 2, inner % 2] = total.astype(BF16)
            return 0

        lax.fori_loop(0, 4, body, 0)

    def sums_send(name, r, q, q_in):
        recv((name, "t2", 1))
        recv((name, "t2", -1))
        add_up(r, q, 2)
        send((name, "q0", 1), q.at[2, 0], q_in.at[5], p_at(1))
        send((name, "q0", -1), q.at[2, 1], q_in.at[6], p_at(-1))
        add_up(r, q, 1)
        send((name, "q2", 1), q.at[1, 1], q_in.at[2], p_cross(1))
        add_up(r, q, 3)
        send((name, "q1", -1), q.at[3, 0], q_in.at[1], p_at(-1))
        add_up(r, q, 0)
        send((name, "q3"), q.at[0, 1], q_in.at[4], sibling)

    def sums_pass(name, q, q_in):
        recv((name, "q0", 1))
        q[1, 0] = (q[1, 0].astype(F32) + q_in[5].astype(F32)).astype(BF16)
        send((name, "q1", 1), q.at[1, 0], q_in.at[0], p_at(1))
        recv((name, "q0", -1))
        q[3, 1] = (q[3, 1].astype(F32) + q_in[6].astype(F32)).astype(BF16)
        send((name, "q2", -1), q.at[3, 1], q_in.at[3], p_cross(-1))

    def sums_end(name, q, q_in, out):
        recv((name, "q1", 1))
        recv((name, "q1", -1))
        recv((name, "q2", 1))
        recv((name, "q2", -1))
        recv((name, "q3"))
        for k in range(2):
            out[k, mine] = (q[0, 0, k].astype(F32) + q_in[0, k].astype(F32) + q_in[1, k].astype(F32)).astype(BF16)
            out[k, others] = (
                q_in[2, k].astype(F32) + q_in[3, k].astype(F32) + q_in[4, k].astype(F32)
            ).astype(BF16)

    def acc_first():
        loads[("w", 0)].wait()

        def body(i, _):
            rows = pl.ds(i * 256, 256)
            acc[rows] = mm(g[0, rows], w[0], NT)
            return 0

        lax.fori_loop(0, 3, body, 0)

    def acc_pair(k):
        def body(i, _):
            rows = pl.ds(i * 256, 256)
            acc[rows] += mm(g[k, rows], w[k], NT) + mm(g[NZ - k, rows], w[NZ - k], NT)
            return 0

        lax.fori_loop(0, 3, body, 0)

    def both(a, b):
        return jnp.concatenate([a, b], axis=0)

    def side():
        recv(("back", "x"))
        recv(("d", "pick"))
        for b in range(NB):
            rows = block(b)
            panel, inner = both(dh[0, b], dx[b]), both(back[rank_rows(0, b)], back_x[rank_rows(0, b)])
            acc[rows] += mm(inner, panel, TN)

    def last_gather():
        recv(("ag", True, 3, 0))
        recv(("ag", False, 3, 1))

        def body(i, _):
            rows = pl.ds(i * 256, 256)
            gt[rows] = (acc[rows] + mm(g[4, rows], w[4], NT)).astype(BF16)
            return 0

        lax.fori_loop(0, 3, body, 0)

    def lift():
        recv(("low", "x"))
        recv(("u", "pick"))
        for b in range(NB):
            panel, inner = both(uh[0, b], ux[b]), both(low[rank_rows(0, b)], low_x[rank_rows(0, b)])
            rows = block(b)
            kv_acc[rows] = mm(tok[0, rows], w[0]) + 0.5 * mm(inner, panel, TN)

    def last_sum():
        for h in (0, 1):
            recv(("rs", True, 3, h))
            recv(("rs", False, 3, h))
            for b in range(h * 3, h * 3 + 3):
                rows = block(b)
                total = kv_acc[rows] + rs_right[3, rows].astype(F32) + rs_left[3, rows].astype(F32)
                kv[rows] = (live(b) * total).astype(BF16)

    def start():
        for h in (0, 1):
            ag_send(0, h, True)
            ag_send(0, h, False)
        send(("u", "f0"), up_in.at[:, others], au.at[0, 0, 1], sibling)
        send("f0i", ints.at[0, 0], ints.at[0, 1], sibling)
        loads["u"].wait()
        f1_send("u", au, 0)
        send(("d", "f0"), down_in.at[:, others], ad.at[0, 0, 1], sibling)
        loads["d"].wait()
        f1_send("d", ad, 0)
        send("xg", g.at[0], g_sib, sibling)

    def rs_begin():
        loads["tok"].wait()
        loads[("w", 4)].wait()
        rs_start(0, 0, True)
        rs_start(0, 1, False)
        loads[("w", 3)].wait()
        rs_start(1, 1, True)
        loads[("w", 5)].wait()
        rs_start(1, 0, False)
        send("xtok", tok.at[0], tok.at[1], sibling)
        for k in (2, 6, 1, 7):
            loads[("w", k)].wait()

    def ints_0():
        recv("f0i")
        send(("i", 1), ints.at[0], ints.at[3], q_at(1))
        send(("i", -1), ints.at[0], ints.at[1], q_at(-1))

    def ints_1():
        recv(("i", 1))
        send(("i", 2), ints.at[3], ints.at[2], q_at(1))

    def ints_2():
        recv(("i", -1))
        recv(("i", 2))
        to_smem = pltpu.make_async_copy(ints, ints_smem, copy_sem)
        to_smem.start()
        to_smem.wait()

    start()
    fetch_0("u", au)
    fetch_0("d", ad)
    fetch_1("u", au)
    fetch_3("u", au)
    ints_0()
    fetch_2("u", au)
    rs_begin()
    ag_pass(0, 1)
    fetch_1("d", ad)
    fetch_5("u", au)
    fetch_4("u", au)
    ints_1()
    ints_2()
    back_begin()
    fetch_4("d", ad)
    fill_table()
    ag_pass(0, 0)
    fetch_2("d", ad)
    fetch_5("d", ad)
    fetch_3("d", ad)
    ag_pass(1, 1)
    acc_first()
    sum_gather("back", back_part, back_recv, back, 0.5)
    low_begin()
    ag_pass(1, 0)
    down_terms()
    rs_pass(1, 1)
    rs_pass(1, 0)
    sum_gather("low", low_part, low_recv, low, 1.0)
    terms_pass("d", rd)
    rs_pass(2, 1)
    ag_pass(2, 1)
    ag_pass(2, 0)
    up_terms()
    acc_pair(1)
    acc_pair(2)
    rs_pass(2, 0)
    sums_send("d", rd, qd, qd_in)
    side()
    rs_pass(3, 1)
    terms_pass("u", ru)
    acc_pair(3)
    rs_pass(3, 0)
    sums_pass("d", qd, qd_in)
    last_gather()
    sums_send("u", ru, qu, qu_in)
    sums_pass("u", qu, qu_in)
    lift()
    sums_end("d", qd, qd_in, gd)
    sums_end("u", qu, qu_in, gu)
    last_sum()

    for copy in sent.values():
        copy.wait_send()


def local(tokens, frozen_weight, cotangent, down_maps, up_maps, stored_row, tenants, padding):
    shape = jax.ShapeDtypeStruct
    smem, anywhere = pl.BlockSpec(memory_space=pltpu.SMEM), pl.BlockSpec(memory_space=pl.ANY)
    vmem = pltpu.VMEM
    inside = pl.BlockSpec(memory_space=vmem)
    shapes = (
        shape((ROWS, COLS), BF16), shape((ROWS, FEAT), BF16),
        shape((2, RANK, FEAT), BF16), shape((2, RANK, COLS), BF16),
    )
    kv, gt, gd, gu = pl.pallas_call(
        kernel,
        name="projections",
        out_shape=tuple(vmem(s.shape, s.dtype) for s in shapes),
        in_specs=[smem] * 3 + [pl.BlockSpec(memory_space=pltpu.HBM)] * 5,
        out_specs=[inside] * 4,
        scratch_shapes=[
            vmem((2, ROWS, FEAT), BF16),
            vmem((NZ, FEAT, COLS), BF16),
            vmem((NZ, ROWS, COLS), BF16),
            vmem((ROWS, COLS), BF16),
            vmem((ROWS, FEAT), F32),
            vmem((ROWS, COLS), F32),
            vmem((4, ROWS, COLS), BF16),
            vmem((4, ROWS, COLS), BF16),
            vmem((4, HALF, COLS), BF16),
            vmem((4, 4, 2, 2, HR, FEAT), BF16),
            vmem((4, 4, 2, 2, HR, COLS), BF16),
            vmem((2, NB, HR, FEAT), BF16),
            vmem((2, NB, HR, COLS), BF16),
            vmem((NB, HR, FEAT), BF16),
            vmem((NB, HR, COLS), BF16),
            vmem((4, 2, 8, 128), I32),
            pltpu.SMEM((4, 2, 8, 128), I32),
            pltpu.SMEM((16, 8), I32),
            vmem((2 * NB * HR, BR), BF16),
            vmem((NZ, 48, BR), BF16),
            vmem((2 * NB * HR, BR), BF16),
            vmem((NB * HR, BR), BF16),
            vmem((2 * NB * HR, BR), BF16),
            vmem((NZ, 48, BR), BF16),
            vmem((2 * NB * HR, BR), BF16),
            vmem((NB * HR, BR), BF16),
            vmem((49, HR, FEAT), BF16),
            vmem((49, HR, COLS), BF16),
            vmem((4, 2, 2, HR, FEAT), BF16),
            vmem((4, 2, 2, HR, COLS), BF16),
            vmem((7, 2, HR, FEAT), BF16),
            vmem((7, 2, HR, COLS), BF16),
            pltpu.SemaphoreType.DMA((N_SEM,)),
            pltpu.SemaphoreType.DMA((N_SEM,)),
            pltpu.SemaphoreType.DMA((16,)),
            pltpu.SemaphoreType.DMA,
        ],
        compiler_params=pltpu.CompilerParams(
            collective_id=0, has_side_effects=True, vmem_limit_bytes=60 * 2**20
        ),
    )(
        stored_row, tenants, padding, tokens, frozen_weight, cotangent,
        jnp.swapaxes(down_maps, 1, 2), up_maps,
    )
    return kv, gt, jnp.swapaxes(gd, 1, 2), gu


def solution(mesh):
    placed = (
        P("dp", "tensor"),
        P("tensor", None),
        P("dp", "tensor"),
        P("dp", "tensor", None),
        P("dp", None, "tensor"),
        P(),
        P("dp"),
        P("dp"),
    )
    return jax.shard_map(
        local,
        mesh=mesh,
        in_specs=placed,
        out_specs=(
            P("dp", "tensor"),
            P("dp", "tensor"),
            P("dp", "tensor", None),
            P("dp", None, "tensor"),
        ),
        check_vma=False,
    )
```

```python
import jax
import jax.numpy as jnp
from jax import lax
from jax.experimental import pallas as pl
from jax.experimental.pallas import tpu as pltpu
from jax.sharding import PartitionSpec as P

MESH = pl.DeviceIdType.MESH
F32, BF16, I32 = jnp.float32, jnp.bfloat16, jnp.int32
NT = (((1,), (1,)), ((), ()))
TN = (((0,), (0,)), ((), ()))
NZ, NB, BR = 8, 6, 128
ROWS, PIECES, PIECE = 768, 4, 192
FEAT, COLS, RANK, HR = 1024, 256, 64, 32
N_SEM = 200


def mm(a, b, dims=None):
    if dims is None:
        return jnp.dot(a, b, preferred_element_type=F32)
    return lax.dot_general(a, b, dims, preferred_element_type=F32)


def kernel(
    stored, tenants, padding, tok_in, w_in, cot_in, down_in, up_in,
    kv, gt, gd, gu,
    tok, w, g, g_sib, acc, kv_acc, rs_right, rs_left, rs_first,
    ad, au, dh, uh, dx, ux, ints, ints_smem, table,
    low_part, low_recv, low, low_x, back_part, back_recv, back, back_x,
    rd, ru, qd, qu, qd_in, qu_in,
    send_sem, recv_sem, load_sem, copy_sem,
):
    dp, z = lax.axis_index("dp"), lax.axis_index("tensor")
    y, x, c = dp // 8, (dp // 2) % 4, dp % 2
    mp, mq = (1 - c) * x + c * y, (1 - c) * y + c * x

    def z_at(step):
        return (dp, (z + step + NZ) % NZ)

    def chip_at(dy, dx_, core):
        return (((y + dy + 4) % 4) * 8 + ((x + dx_ + 4) % 4) * 2 + core, z)

    def p_at(step):
        return chip_at(c * step, (1 - c) * step, c)

    def q_at(step):
        return chip_at((1 - c) * step, c * step, c)

    def p_cross(step):
        return chip_at(c * step, (1 - c) * step, 1 - c)

    def q_cross(step):
        return chip_at((1 - c) * step, c * step, 1 - c)

    sibling = (dp + 1 - 2 * c, z)
    sent = {}

    def send(key, src, dst, device):
        n = len(sent)
        copy = pltpu.make_async_remote_copy(
            src_ref=src, dst_ref=dst, send_sem=send_sem.at[n], recv_sem=recv_sem.at[n],
            device_id=device, device_id_type=MESH,
        )
        copy.start()
        sent[key] = copy

    arrived = set()

    def recv(key):
        if key not in arrived:
            arrived.add(key)
            sent[key].wait_recv()

    loads = {}

    def load(key, src, dst):
        loads[key] = pltpu.make_async_copy(src, dst, load_sem.at[len(loads)])
        loads[key].start()

    loaded = set()

    def wait_load(key):
        if key not in loaded:
            loaded.add(key)
            loads[key].wait()

    def wait_w(k):
        wait_load(("w", k))

    mine, others = pl.ds(c * HR, HR), pl.ds((1 - c) * HR, HR)
    load("g", cot_in, g.at[0])
    load("u", up_in.at[:, mine], au.at[0, 0, 0])
    load("d", down_in.at[:, mine], ad.at[0, 0, 0])
    load("tok", tok_in, tok.at[0])
    for k in (4, 3, 5, 0, 2, 6, 1, 7):
        load(("w", k), w_in.at[:, pl.ds(((z + k) % NZ) * COLS, COLS)], w.at[k])

    barrier = pltpu.get_barrier_semaphore()
    friends = [z_at(k) for k in range(1, NZ)] + [p_at(1), p_at(-1), q_at(1), q_at(-1), sibling]
    friends += [q_cross(1), q_cross(-1)]
    for friend in friends:
        pl.semaphore_signal(barrier, inc=1, device_id=friend, device_id_type=MESH)

    lane = lax.broadcasted_iota(I32, (8, 128), 1)
    tile = jnp.zeros((8, 128), I32)
    for b in range(NB):
        tile = jnp.where(lane == b, stored[tenants[b]], tile)
    ints[0, 0] = tile

    position = lax.broadcasted_iota(I32, (BR, 1), 0)

    def live(b):
        return (position < BR - padding[b]).astype(F32)

    wait_load("g")
    for b in range(NB):
        rows = pl.ds(b * BR, BR)
        g[0, rows] = (g[0, rows].astype(F32) * live(b)).astype(BF16)

    pl.semaphore_wait(barrier, len(friends))

    half = [pl.ds(h * PIECE, PIECE) for h in range(PIECES)]

    def goes_right(h):
        return h < PIECES // 2

    def ag_send(step, h, right):
        src, dst = ((-step) % NZ, (-step - 1) % NZ) if right else (step, step + 1)
        send(("ag", right, step, h), g.at[src, half[h]], g.at[dst, half[h]], z_at(1 if right else -1))

    def ag_pass(step, h):
        for right in (True, False):
            recv(("ag", right, step, h))
            if step < 2 or goes_right(h) == right:
                ag_send(step + 1, h, right)

    def partial(k, h):
        return mm(tok[0, half[h]], w[k])

    def rs_start(h):
        wait_load("tok")
        for right in (True, False):
            step = 0 if goes_right(h) == right else 1
            k = (4 - step) if right else (4 + step)
            wait_w(k)
            slot = 0 if right else 1
            rs_first[slot, half[h]] = partial(k, h).astype(BF16)
            dst = rs_right if right else rs_left
            send(("rs", right, step, h), rs_first.at[slot, half[h]], dst.at[step, half[h]], z_at(1 if right else -1))

    def rs_pass(step, h):
        wait_w(4 - step)
        wait_w(4 + step)
        for right in (True, False):
            if step == 1 and goes_right(h) != right:
                continue
            k = (4 - step) if right else (4 + step)
            buf = rs_right if right else rs_left
            own = partial(k, h)
            recv(("rs", right, step - 1, h))
            buf[step - 1, half[h]] = (buf[step - 1, half[h]].astype(F32) + own).astype(BF16)
            send(("rs", right, step, h), buf.at[step - 1, half[h]], buf.at[step, half[h]], z_at(1 if right else -1))

    def f1_send(name, a, r):
        send((name, "f1", 1, r), a.at[0, 0, r], a.at[0, 3, r], p_at(1))
        send((name, "f1", -1, r), a.at[0, 0, r], a.at[0, 1, r], p_at(-1))

    def f1_pass(name, a):
        recv((name, "f1", 1, 0))
        send((name, "f1x", 1), a.at[0, 3, 0], a.at[0, 2, 0], p_at(1))
        recv((name, "f1", -1, 1))
        send((name, "f1x", -1), a.at[0, 1, 1], a.at[0, 2, 1], p_at(-1))
        recv((name, "f1", 1, 1))
        recv((name, "f1", -1, 0))

    def f1_end(name):
        recv((name, "f1x", 1))
        recv((name, "f1x", -1))

    def f2_send(name, a, rp):
        send((name, "f2", 1, rp), a.at[0, rp], a.at[3, rp], q_at(1))
        send((name, "f2", -1, rp), a.at[0, rp], a.at[1, rp], q_at(-1))

    def f2_pass(name, a, rp):
        recv((name, "f2", 1, rp))
        send((name, "f2x", 1, rp), a.at[3, rp, 0], a.at[2, rp, 0], q_at(1))
        recv((name, "f2", -1, rp))
        send((name, "f2x", -1, rp), a.at[1, rp, 1], a.at[2, rp, 1], q_at(-1))

    def f2_end(name):
        for rp in range(4):
            recv((name, "f2x", 1, rp))
            recv((name, "f2x", -1, rp))

    def fetch_0(name, a):
        recv((name, "f0"))
        f1_send(name, a, 1)
        f2_send(name, a, 0)

    def fetch_1(name, a):
        f1_pass(name, a)
        f2_send(name, a, 3)
        f2_send(name, a, 1)

    def fetch_2(name, a):
        f1_end(name)
        f2_send(name, a, 2)

    def fetch_3(name, a):
        f2_pass(name, a, 0)

    def fetch_4(name, a):
        f2_pass(name, a, 3)
        f2_pass(name, a, 1)

    def fetch_5(name, a):
        f2_pass(name, a, 2)

    def place(slot):
        chip, inner = slot // 4, slot % 4
        cy, cx = chip // 4, chip % 4
        rq = ((1 - c) * cy + c * cx - mq + 4) % 4
        rp = ((1 - c) * cx + c * cy - mp + 4) % 4
        return rq, rp, (inner // 2 + c) % 2, inner % 2

    def pick(name, a, picked, out):
        f2_end(name)
        for r in (1, 0):
            for b in range(NB):
                rq, rp, core, inner = place(ints_smem[0, r, 0, b])
                picked[r, b] = a[rq, rp, core, inner]
        send((name, "pick"), picked.at[1], out, sibling)

    def sum_scatter(name, part, got):
        for k in range(1, NZ):
            rows = pl.ds(((z + k) % NZ) * 48, 48)
            send((name, "s", k), part.at[rows], got.at[k], z_at(k))

    def sum_gather(name, part, got, total, scale):
        own = pl.ds(z * 48, 48)
        value = part[own].astype(F32)
        for k in range(1, NZ):
            recv((name, "s", k))
            value = value + got[k].astype(F32)
        total[own] = (value * scale).astype(BF16)
        for k in range(1, NZ):
            send((name, "g", k), total.at[own], total.at[own], z_at(k))

    def sum_end(name, total, out):
        for k in range(1, NZ):
            recv((name, "g", k))
        send((name, "x"), total.at[pl.ds(NB * HR, NB * HR)], out, sibling)

    def rank_rows(r, b):
        return pl.ds((r * NB + b) * HR, HR)

    def block(b):
        return pl.ds(b * BR, BR)

    def back_begin():
        pick("u", au, uh, ux)
        recv("xg")
        for b in range(NB):
            back_part[rank_rows(0, b)] = mm(uh[0, b], g[0, block(b)], NT).astype(BF16)
            back_part[rank_rows(1, b)] = mm(uh[1, b], g_sib[block(b)], NT).astype(BF16)
        sum_scatter("back", back_part, back_recv)

    def low_begin():
        pick("d", ad, dh, dx)
        recv("xtok")
        for r in (0, 1):
            for b in range(NB):
                low_part[rank_rows(r, b)] = mm(dh[r, b], tok[r, block(b)], NT).astype(BF16)
        sum_scatter("low", low_part, low_recv)

    def terms_send(name, r, core):
        src = r.at[pl.ds(core * NB, NB)]
        send((name, "t1", 1, core), src, r.at[pl.ds(36 + core * NB, NB)], q_at(1))
        send((name, "t1", -1, core), src, r.at[pl.ds(12 + core * NB, NB)], q_at(-1))

    def down_terms():
        sum_end("back", back, back_x)
        recv("xtok")
        for r in (0, 1):
            for b in range(NB):
                rd[r * NB + b] = mm(back[rank_rows(r, b)], tok[r, block(b)]).astype(BF16)
            terms_send("d", rd, r)

    def up_terms():
        sum_end("low", low, low_x)
        for b in range(NB):
            ru[b] = (0.5 * mm(low[rank_rows(0, b)], g[0, block(b)])).astype(BF16)
        terms_send("u", ru, 0)
        for b in range(NB):
            ru[NB + b] = (0.5 * mm(low[rank_rows(1, b)], g_sib[block(b)])).astype(BF16)
        terms_send("u", ru, 1)

    def terms_pass(name, r):
        recv((name, "t1", 1, 0))
        send((name, "t2", 1), r.at[pl.ds(36, NB)], r.at[pl.ds(24, NB)], q_at(1))
        recv((name, "t1", -1, 1))
        send((name, "t2", -1), r.at[pl.ds(12 + NB, NB)], r.at[pl.ds(24 + NB, NB)], q_at(-1))
        recv((name, "t1", 1, 1))
        recv((name, "t1", -1, 0))

    def fill_table():
        rd[48] = jnp.zeros((HR, FEAT), BF16)
        ru[48] = jnp.zeros((HR, COLS), BF16)

        def body(j, _):
            pj, core = (mp + j // 4) % 4, (j // 2 + c) % 2
            slot = (((1 - c) * mq + c * pj) * 4 + (1 - c) * pj + c * mq) * 4 + core * 2 + j % 2
            for i in range(4):
                for r in range(2):
                    entry = I32(48)
                    for b in range(NB):
                        entry = jnp.where(ints_smem[i, r, 0, b] == slot, (i * 2 + r) * NB + b, entry)
                    table[j, i * 2 + r] = entry
            return 0

        lax.fori_loop(0, 16, body, 0)

    def add_up(r, q, j):
        def body(inner, _):
            total = r[table[j * 4 + inner, 0]].astype(F32)
            for d in range(1, 8):
                total = total + r[table[j * 4 + inner, d]].astype(F32)
            q[j, inner // 2, inner % 2] = total.astype(BF16)
            return 0

        lax.fori_loop(0, 4, body, 0)

    def sums_send(name, r, q, q_in):
        recv((name, "t2", 1))
        recv((name, "t2", -1))
        add_up(r, q, 2)
        send((name, "q0", 1), q.at[2, 0], q_in.at[5], p_at(1))
        send((name, "q0", -1), q.at[2, 1], q_in.at[6], p_at(-1))
        add_up(r, q, 1)
        send((name, "q2", 1), q.at[1, 1], q_in.at[2], p_cross(1))
        add_up(r, q, 3)
        send((name, "q1", -1), q.at[3, 0], q_in.at[1], p_at(-1))
        add_up(r, q, 0)
        send((name, "q3"), q.at[0, 1], q_in.at[4], sibling)

    def sums_pass(name, q, q_in):
        recv((name, "q0", 1))
        q[1, 0] = (q[1, 0].astype(F32) + q_in[5].astype(F32)).astype(BF16)
        send((name, "q1", 1), q.at[1, 0], q_in.at[0], p_at(1))
        recv((name, "q0", -1))
        q[3, 1] = (q[3, 1].astype(F32) + q_in[6].astype(F32)).astype(BF16)
        send((name, "q2", -1), q.at[3, 1], q_in.at[3], p_cross(-1))

    def sums_end(name, q, q_in, out):
        recv((name, "q1", 1))
        recv((name, "q1", -1))
        recv((name, "q2", 1))
        recv((name, "q2", -1))
        recv((name, "q3"))
        for k in range(2):
            out[k, mine] = (q[0, 0, k].astype(F32) + q_in[0, k].astype(F32) + q_in[1, k].astype(F32)).astype(BF16)
            out[k, others] = (
                q_in[2, k].astype(F32) + q_in[3, k].astype(F32) + q_in[4, k].astype(F32)
            ).astype(BF16)

    def acc_first():
        wait_w(0)

        def body(i, _):
            rows = pl.ds(i * 256, 256)
            acc[rows] = mm(g[0, rows], w[0], NT)
            return 0

        lax.fori_loop(0, 3, body, 0)

    def acc_pair(k):
        wait_w(k)
        wait_w(NZ - k)

        def body(i, _):
            rows = pl.ds(i * 256, 256)
            acc[rows] += mm(g[k, rows], w[k], NT) + mm(g[NZ - k, rows], w[NZ - k], NT)
            return 0

        lax.fori_loop(0, 3, body, 0)

    def both(a, b):
        return jnp.concatenate([a, b], axis=0)

    def side():
        recv(("back", "x"))
        recv(("d", "pick"))
        for b in range(NB):
            rows = block(b)
            panel, inner = both(dh[0, b], dx[b]), both(back[rank_rows(0, b)], back_x[rank_rows(0, b)])
            acc[rows] += mm(inner, panel, TN)

    def last_gather():
        wait_w(4)
        for h in range(PIECES):
            recv(("ag", goes_right(h), 3, h))

        def body(i, _):
            rows = pl.ds(i * 256, 256)
            gt[rows] = (acc[rows] + mm(g[4, rows], w[4], NT)).astype(BF16)
            return 0

        lax.fori_loop(0, 3, body, 0)

    def lift():
        wait_w(0)
        wait_load("tok")
        recv(("low", "x"))
        recv(("u", "pick"))
        for b in range(NB):
            panel, inner = both(uh[0, b], ux[b]), both(low[rank_rows(0, b)], low_x[rank_rows(0, b)])
            rows = block(b)
            kv_acc[rows] = mm(tok[0, rows], w[0]) + 0.5 * mm(inner, panel, TN)

    def last_sum():
        done = 0
        for h in range(PIECES):
            recv(("rs", True, 3, h))
            recv(("rs", False, 3, h))
            for b in range(done, (h + 1) * NB // PIECES):
                rows = block(b)
                total = kv_acc[rows] + rs_right[3, rows].astype(F32) + rs_left[3, rows].astype(F32)
                kv[rows] = (live(b) * total).astype(BF16)
            done = (h + 1) * NB // PIECES

    def ag_start(h):
        ag_send(0, h, True)
        ag_send(0, h, False)

    def up_start():
        send(("u", "f0"), up_in.at[:, others], au.at[0, 0, 1], sibling)
        send("f0i", ints.at[0, 0], ints.at[0, 1], sibling)
        wait_load("u")
        f1_send("u", au, 0)

    def down_start():
        send(("d", "f0"), down_in.at[:, others], ad.at[0, 0, 1], sibling)
        wait_load("d")
        f1_send("d", ad, 0)

    def grad_rows_out():
        send("xg", g.at[0], g_sib, sibling)

    def tokens_out():
        wait_load("tok")
        send("xtok", tok.at[0], tok.at[1], sibling)

    def ints_0():
        recv("f0i")
        send(("i", 1), ints.at[0], ints.at[3], q_at(1))
        send(("i", -1), ints.at[0], ints.at[1], q_at(-1))

    def ints_1():
        recv(("i", 1))
        send(("i", 2), ints.at[3], ints.at[2], q_at(1))

    def ints_2():
        recv(("i", -1))
        recv(("i", 2))
        to_smem = pltpu.make_async_copy(ints, ints_smem, copy_sem)
        to_smem.start()
        to_smem.wait()

    ag_start(2)
    ag_start(3)
    up_start()
    fetch_0("u", au)
    down_start()
    ints_0()
    rs_start(2)
    ag_start(1)
    fetch_1("u", au)
    fetch_3("u", au)
    fetch_2("u", au)
    ag_start(0)
    grad_rows_out()
    rs_start(0)
    fetch_0("d", ad)
    ints_1()
    ag_pass(0, 3)
    fetch_4("u", au)
    rs_start(1)
    rs_start(3)
    tokens_out()
    acc_first()
    rs_pass(1, 2)
    fetch_5("u", au)
    fetch_1("d", ad)
    ints_2()
    back_begin()
    ag_pass(0, 1)
    fetch_3("d", ad)
    rs_pass(1, 1)
    rs_pass(1, 0)
    fetch_2("d", ad)
    fetch_4("d", ad)
    rs_pass(1, 3)
    sum_gather("back", back_part, back_recv, back, 0.5)
    ag_pass(0, 2)
    ag_pass(0, 0)
    rs_pass(2, 2)
    fetch_5("d", ad)
    rs_pass(2, 1)
    low_begin()
    down_terms()
    ag_pass(1, 2)
    fill_table()
    ag_pass(1, 0)
    side()
    sum_gather("low", low_part, low_recv, low, 1.0)
    rs_pass(3, 2)
    rs_pass(2, 3)
    terms_pass("d", rd)
    ag_pass(1, 1)
    acc_pair(1)
    ag_pass(1, 3)
    acc_pair(2)
    up_terms()
    rs_pass(2, 0)
    ag_pass(2, 0)
    sums_send("d", rd, qd, qd_in)
    terms_pass("u", ru)
    ag_pass(2, 3)
    ag_pass(2, 2)
    rs_pass(3, 1)
    sums_pass("d", qd, qd_in)
    ag_pass(2, 1)
    acc_pair(3)
    sums_send("u", ru, qu, qu_in)
    rs_pass(3, 0)
    rs_pass(3, 3)
    sums_end("d", qd, qd_in, gd)
    sums_pass("u", qu, qu_in)
    last_gather()
    sums_end("u", qu, qu_in, gu)
    lift()
    last_sum()

    for copy in sent.values():
        copy.wait_send()


def local(tokens, frozen_weight, cotangent, down_maps, up_maps, stored_row, tenants, padding):
    shape = jax.ShapeDtypeStruct
    smem, anywhere = pl.BlockSpec(memory_space=pltpu.SMEM), pl.BlockSpec(memory_space=pl.ANY)
    vmem = pltpu.VMEM
    inside = pl.BlockSpec(memory_space=vmem)
    shapes = (
        shape((ROWS, COLS), BF16), shape((ROWS, FEAT), BF16),
        shape((2, RANK, FEAT), BF16), shape((2, RANK, COLS), BF16),
    )
    kv, gt, gd, gu = pl.pallas_call(
        kernel,
        name="projections",
        out_shape=tuple(vmem(s.shape, s.dtype) for s in shapes),
        in_specs=[smem] * 3 + [pl.BlockSpec(memory_space=pltpu.HBM)] * 5,
        out_specs=[inside] * 4,
        scratch_shapes=[
            vmem((2, ROWS, FEAT), BF16),
            vmem((NZ, FEAT, COLS), BF16),
            vmem((NZ, ROWS, COLS), BF16),
            vmem((ROWS, COLS), BF16),
            vmem((ROWS, FEAT), F32),
            vmem((ROWS, COLS), F32),
            vmem((4, ROWS, COLS), BF16),
            vmem((4, ROWS, COLS), BF16),
            vmem((2, ROWS, COLS), BF16),
            vmem((4, 4, 2, 2, HR, FEAT), BF16),
            vmem((4, 4, 2, 2, HR, COLS), BF16),
            vmem((2, NB, HR, FEAT), BF16),
            vmem((2, NB, HR, COLS), BF16),
            vmem((NB, HR, FEAT), BF16),
            vmem((NB, HR, COLS), BF16),
            vmem((4, 2, 8, 128), I32),
            pltpu.SMEM((4, 2, 8, 128), I32),
            pltpu.SMEM((16, 8), I32),
            vmem((2 * NB * HR, BR), BF16),
            vmem((NZ, 48, BR), BF16),
            vmem((2 * NB * HR, BR), BF16),
            vmem((NB * HR, BR), BF16),
            vmem((2 * NB * HR, BR), BF16),
            vmem((NZ, 48, BR), BF16),
            vmem((2 * NB * HR, BR), BF16),
            vmem((NB * HR, BR), BF16),
            vmem((49, HR, FEAT), BF16),
            vmem((49, HR, COLS), BF16),
            vmem((4, 2, 2, HR, FEAT), BF16),
            vmem((4, 2, 2, HR, COLS), BF16),
            vmem((7, 2, HR, FEAT), BF16),
            vmem((7, 2, HR, COLS), BF16),
            pltpu.SemaphoreType.DMA((N_SEM,)),
            pltpu.SemaphoreType.DMA((N_SEM,)),
            pltpu.SemaphoreType.DMA((16,)),
            pltpu.SemaphoreType.DMA,
        ],
        compiler_params=pltpu.CompilerParams(
            collective_id=0, has_side_effects=True, vmem_limit_bytes=60 * 2**20
        ),
    )(
        stored_row, tenants, padding, tokens, frozen_weight, cotangent,
        jnp.swapaxes(down_maps, 1, 2), up_maps,
    )
    return kv, gt, jnp.swapaxes(gd, 1, 2), gu


def solution(mesh):
    placed = (
        P("dp", "tensor"),
        P("tensor", None),
        P("dp", "tensor"),
        P("dp", "tensor", None),
        P("dp", None, "tensor"),
        P(),
        P("dp"),
        P("dp"),
    )
    return jax.shard_map(
        local,
        mesh=mesh,
        in_specs=placed,
        out_specs=(
            P("dp", "tensor"),
            P("dp", "tensor"),
            P("dp", "tensor", None),
            P("dp", None, "tensor"),
        ),
        check_vma=False,
    )
```

```python
import jax
import jax.numpy as jnp
from jax import lax
from jax.experimental import pallas as pl
from jax.experimental.pallas import tpu as pltpu
from jax.sharding import PartitionSpec as P

MESH = pl.DeviceIdType.MESH
F32, BF16, I32 = jnp.float32, jnp.bfloat16, jnp.int32
NT = (((1,), (1,)), ((), ()))
TN = (((0,), (0,)), ((), ()))
NZ, NB, BR = 8, 6, 128
ROWS, PIECES, PIECE = 768, 4, 192
FEAT, COLS, RANK, HR = 1024, 256, 64, 32
N_SEM = 200


def mm(a, b, dims=None):
    if dims is None:
        return jnp.dot(a, b, preferred_element_type=F32)
    return lax.dot_general(a, b, dims, preferred_element_type=F32)


def kernel(
    stored, tenants, padding, tok_in, w_in, cot_in, down_in, up_in,
    kv, gt, gd, gu,
    tok, w, g, g_sib, acc, kv_acc, rs_right, rs_left, rs_first,
    ad, au, dh, uh, dx, ux, ints, ints_smem, table,
    low_part, low_recv, low, low_x, back_part, back_recv, back, back_x,
    rd, ru, qd, qu, qd_in, qu_in,
    send_sem, recv_sem, load_sem, copy_sem, far_sem,
):
    dp, z = lax.axis_index("dp"), lax.axis_index("tensor")
    y, x, c = dp // 8, (dp // 2) % 4, dp % 2
    mp, mq = (1 - c) * x + c * y, (1 - c) * y + c * x

    def z_at(step):
        return (dp, (z + step + NZ) % NZ)

    def chip_at(dy, dx_, core):
        return (((y + dy + 4) % 4) * 8 + ((x + dx_ + 4) % 4) * 2 + core, z)

    def p_at(step):
        return chip_at(c * step, (1 - c) * step, c)

    def q_at(step):
        return chip_at((1 - c) * step, c * step, c)

    def p_cross(step):
        return chip_at(c * step, (1 - c) * step, 1 - c)

    def q_cross(step):
        return chip_at((1 - c) * step, c * step, 1 - c)

    sibling = (dp + 1 - 2 * c, z)
    sent = {}

    def send(key, src, dst, device):
        n = len(sent)
        copy = pltpu.make_async_remote_copy(
            src_ref=src, dst_ref=dst, send_sem=send_sem.at[n], recv_sem=recv_sem.at[n],
            device_id=device, device_id_type=MESH,
        )
        copy.start()
        sent[key] = copy

    arrived = set()

    def recv(key):
        if key not in arrived:
            arrived.add(key)
            sent[key].wait_recv()

    barrier = pltpu.get_barrier_semaphore()
    friends = [z_at(1), z_at(-1)] + [p_at(1), p_at(-1), q_at(1), q_at(-1), sibling]
    friends += [q_cross(1), q_cross(-1)]
    for friend in friends:
        pl.semaphore_signal(barrier, inc=1, device_id=friend, device_id_type=MESH)

    loads = {}

    def load(key, src, dst):
        loads[key] = pltpu.make_async_copy(src, dst, load_sem.at[len(loads)])
        loads[key].start()

    loaded = set()

    def wait_load(key):
        if key not in loaded:
            loaded.add(key)
            loads[key].wait()

    def wait_w(k):
        wait_load(("w", k))

    mine, others = pl.ds(c * HR, HR), pl.ds((1 - c) * HR, HR)
    load("g", cot_in, g.at[0])
    load("u", up_in.at[:, mine], au.at[0, 0, 0])
    load("d", down_in.at[:, mine], ad.at[0, 0, 0])
    load("tok", tok_in, tok.at[0])
    for k in (4, 3, 5, 0, 2, 6, 1, 7):
        load(("w", k), w_in.at[:, pl.ds(((z + k) % NZ) * COLS, COLS)], w.at[k])

    lane = lax.broadcasted_iota(I32, (8, 128), 1)
    tile = jnp.zeros((8, 128), I32)
    for b in range(NB):
        tile = jnp.where(lane == b, stored[tenants[b]], tile)
    ints[0, 0] = tile

    position = lax.broadcasted_iota(I32, (BR, 1), 0)

    def live(b):
        return (position < BR - padding[b]).astype(F32)

    wait_load("g")
    for b in range(NB):
        rows = pl.ds(b * BR, BR)
        g[0, rows] = (g[0, rows].astype(F32) * live(b)).astype(BF16)

    pl.semaphore_wait(barrier, len(friends))

    def tell(k, step):
        for way in (step, -step):
            pl.semaphore_signal(far_sem.at[k], inc=1, device_id=z_at(way), device_id_type=MESH)

    tell(0, 1)

    half = [pl.ds(h * PIECE, PIECE) for h in range(PIECES)]

    def goes_right(h):
        return h < PIECES // 2

    def ag_send(step, h, right):
        src, dst = ((-step) % NZ, (-step - 1) % NZ) if right else (step, step + 1)
        send(("ag", right, step, h), g.at[src, half[h]], g.at[dst, half[h]], z_at(1 if right else -1))

    def ag_pass(step, h):
        for right in (True, False):
            recv(("ag", right, step, h))
            if step < 2 or goes_right(h) == right:
                ag_send(step + 1, h, right)

    def partial(k, h):
        return mm(tok[0, half[h]], w[k])

    def rs_start(h):
        wait_load("tok")
        for right in (True, False):
            step = 0 if goes_right(h) == right else 1
            k = (4 - step) if right else (4 + step)
            wait_w(k)
            slot = 0 if right else 1
            rs_first[slot, half[h]] = partial(k, h).astype(BF16)
            dst = rs_right if right else rs_left
            send(("rs", right, step, h), rs_first.at[slot, half[h]], dst.at[step, half[h]], z_at(1 if right else -1))

    def rs_pass(step, h):
        wait_w(4 - step)
        wait_w(4 + step)
        for right in (True, False):
            if step == 1 and goes_right(h) != right:
                continue
            k = (4 - step) if right else (4 + step)
            buf = rs_right if right else rs_left
            own = partial(k, h)
            recv(("rs", right, step - 1, h))
            buf[step - 1, half[h]] = (buf[step - 1, half[h]].astype(F32) + own).astype(BF16)
            send(("rs", right, step, h), buf.at[step - 1, half[h]], buf.at[step, half[h]], z_at(1 if right else -1))

    def f1_send(name, a, r):
        send((name, "f1", 1, r), a.at[0, 0, r], a.at[0, 3, r], p_at(1))
        send((name, "f1", -1, r), a.at[0, 0, r], a.at[0, 1, r], p_at(-1))

    def f1_pass(name, a):
        recv((name, "f1", 1, 0))
        send((name, "f1x", 1), a.at[0, 3, 0], a.at[0, 2, 0], p_at(1))
        recv((name, "f1", -1, 1))
        send((name, "f1x", -1), a.at[0, 1, 1], a.at[0, 2, 1], p_at(-1))
        recv((name, "f1", 1, 1))
        recv((name, "f1", -1, 0))

    def f1_end(name):
        recv((name, "f1x", 1))
        recv((name, "f1x", -1))

    def f2_send(name, a, rp):
        send((name, "f2", 1, rp), a.at[0, rp], a.at[3, rp], q_at(1))
        send((name, "f2", -1, rp), a.at[0, rp], a.at[1, rp], q_at(-1))

    def f2_pass(name, a, rp):
        recv((name, "f2", 1, rp))
        send((name, "f2x", 1, rp), a.at[3, rp, 0], a.at[2, rp, 0], q_at(1))
        recv((name, "f2", -1, rp))
        send((name, "f2x", -1, rp), a.at[1, rp, 1], a.at[2, rp, 1], q_at(-1))

    def f2_end(name):
        for rp in range(4):
            recv((name, "f2x", 1, rp))
            recv((name, "f2x", -1, rp))

    def fetch_0(name, a):
        recv((name, "f0"))
        f1_send(name, a, 1)
        f2_send(name, a, 0)

    def fetch_1(name, a):
        f1_pass(name, a)
        f2_send(name, a, 3)
        f2_send(name, a, 1)

    def fetch_2(name, a):
        f1_end(name)
        f2_send(name, a, 2)

    def fetch_3(name, a):
        f2_pass(name, a, 0)

    def fetch_4(name, a):
        f2_pass(name, a, 3)
        f2_pass(name, a, 1)

    def fetch_5(name, a):
        f2_pass(name, a, 2)

    def place(slot):
        chip, inner = slot // 4, slot % 4
        cy, cx = chip // 4, chip % 4
        rq = ((1 - c) * cy + c * cx - mq + 4) % 4
        rp = ((1 - c) * cx + c * cy - mp + 4) % 4
        return rq, rp, (inner // 2 + c) % 2, inner % 2

    def pick(name, a, picked, out):
        f2_end(name)
        for r in (1, 0):
            for b in range(NB):
                rq, rp, core, inner = place(ints_smem[0, r, 0, b])
                picked[r, b] = a[rq, rp, core, inner]
        send((name, "pick"), picked.at[1], out, sibling)

    def sum_scatter(name, part, got):
        for k in range(1, NZ):
            rows = pl.ds(((z + k) % NZ) * 48, 48)
            send((name, "s", k), part.at[rows], got.at[k], z_at(k))

    def sum_gather(name, part, got, total, scale):
        own = pl.ds(z * 48, 48)
        value = part[own].astype(F32)
        for k in range(1, NZ):
            recv((name, "s", k))
            value = value + got[k].astype(F32)
        total[own] = (value * scale).astype(BF16)
        for k in range(1, NZ):
            send((name, "g", k), total.at[own], total.at[own], z_at(k))

    def sum_end(name, total, out):
        for k in range(1, NZ):
            recv((name, "g", k))
        send((name, "x"), total.at[pl.ds(NB * HR, NB * HR)], out, sibling)

    def rank_rows(r, b):
        return pl.ds((r * NB + b) * HR, HR)

    def block(b):
        return pl.ds(b * BR, BR)

    def back_begin():
        pick("u", au, uh, ux)
        pl.semaphore_wait(far_sem.at[1], 2)
        recv("xg")
        for b in range(NB):
            back_part[rank_rows(0, b)] = mm(uh[0, b], g[0, block(b)], NT).astype(BF16)
            back_part[rank_rows(1, b)] = mm(uh[1, b], g_sib[block(b)], NT).astype(BF16)
        sum_scatter("back", back_part, back_recv)

    def low_begin():
        pick("d", ad, dh, dx)
        recv("xtok")
        for r in (0, 1):
            for b in range(NB):
                low_part[rank_rows(r, b)] = mm(dh[r, b], tok[r, block(b)], NT).astype(BF16)
        sum_scatter("low", low_part, low_recv)

    def terms_send(name, r, core):
        src = r.at[pl.ds(core * NB, NB)]
        send((name, "t1", 1, core), src, r.at[pl.ds(36 + core * NB, NB)], q_at(1))
        send((name, "t1", -1, core), src, r.at[pl.ds(12 + core * NB, NB)], q_at(-1))

    def down_terms():
        sum_end("back", back, back_x)
        recv("xtok")
        for r in (0, 1):
            for b in range(NB):
                rd[r * NB + b] = mm(back[rank_rows(r, b)], tok[r, block(b)]).astype(BF16)
            terms_send("d", rd, r)

    def up_terms():
        sum_end("low", low, low_x)
        for b in range(NB):
            ru[b] = (0.5 * mm(low[rank_rows(0, b)], g[0, block(b)])).astype(BF16)
        terms_send("u", ru, 0)
        for b in range(NB):
            ru[NB + b] = (0.5 * mm(low[rank_rows(1, b)], g_sib[block(b)])).astype(BF16)
        terms_send("u", ru, 1)

    def terms_pass(name, r):
        recv((name, "t1", 1, 0))
        send((name, "t2", 1), r.at[pl.ds(36, NB)], r.at[pl.ds(24, NB)], q_at(1))
        recv((name, "t1", -1, 1))
        send((name, "t2", -1), r.at[pl.ds(12 + NB, NB)], r.at[pl.ds(24 + NB, NB)], q_at(-1))
        recv((name, "t1", 1, 1))
        recv((name, "t1", -1, 0))

    def fill_table():
        rd[48] = jnp.zeros((HR, FEAT), BF16)
        ru[48] = jnp.zeros((HR, COLS), BF16)

        def body(j, _):
            pj, core = (mp + j // 4) % 4, (j // 2 + c) % 2
            slot = (((1 - c) * mq + c * pj) * 4 + (1 - c) * pj + c * mq) * 4 + core * 2 + j % 2
            for i in range(4):
                for r in range(2):
                    entry = I32(48)
                    for b in range(NB):
                        entry = jnp.where(ints_smem[i, r, 0, b] == slot, (i * 2 + r) * NB + b, entry)
                    table[j, i * 2 + r] = entry
            return 0

        lax.fori_loop(0, 16, body, 0)

    def add_up(r, q, j):
        def body(inner, _):
            total = r[table[j * 4 + inner, 0]].astype(F32)
            for d in range(1, 8):
                total = total + r[table[j * 4 + inner, d]].astype(F32)
            q[j, inner // 2, inner % 2] = total.astype(BF16)
            return 0

        lax.fori_loop(0, 4, body, 0)

    def sums_send(name, r, q, q_in):
        recv((name, "t2", 1))
        recv((name, "t2", -1))
        add_up(r, q, 2)
        send((name, "q0", 1), q.at[2, 0], q_in.at[5], p_at(1))
        send((name, "q0", -1), q.at[2, 1], q_in.at[6], p_at(-1))
        add_up(r, q, 1)
        send((name, "q2", 1), q.at[1, 1], q_in.at[2], p_cross(1))
        add_up(r, q, 3)
        send((name, "q1", -1), q.at[3, 0], q_in.at[1], p_at(-1))
        add_up(r, q, 0)
        send((name, "q3"), q.at[0, 1], q_in.at[4], sibling)

    def sums_pass(name, q, q_in):
        recv((name, "q0", 1))
        q[1, 0] = (q[1, 0].astype(F32) + q_in[5].astype(F32)).astype(BF16)
        send((name, "q1", 1), q.at[1, 0], q_in.at[0], p_at(1))
        recv((name, "q0", -1))
        q[3, 1] = (q[3, 1].astype(F32) + q_in[6].astype(F32)).astype(BF16)
        send((name, "q2", -1), q.at[3, 1], q_in.at[3], p_cross(-1))

    def sums_end(name, q, q_in, out):
        recv((name, "q1", 1))
        recv((name, "q1", -1))
        recv((name, "q2", 1))
        recv((name, "q2", -1))
        recv((name, "q3"))
        for k in range(2):
            out[k, mine] = (q[0, 0, k].astype(F32) + q_in[0, k].astype(F32) + q_in[1, k].astype(F32)).astype(BF16)
            out[k, others] = (
                q_in[2, k].astype(F32) + q_in[3, k].astype(F32) + q_in[4, k].astype(F32)
            ).astype(BF16)

    def acc_first():
        wait_w(0)

        def body(i, _):
            rows = pl.ds(i * 256, 256)
            acc[rows] = mm(g[0, rows], w[0], NT)
            return 0

        lax.fori_loop(0, 3, body, 0)

    def acc_pair(k):
        wait_w(k)
        wait_w(NZ - k)

        def body(i, _):
            rows = pl.ds(i * 256, 256)
            acc[rows] += mm(g[k, rows], w[k], NT) + mm(g[NZ - k, rows], w[NZ - k], NT)
            return 0

        lax.fori_loop(0, 3, body, 0)

    def both(a, b):
        return jnp.concatenate([a, b], axis=0)

    def side():
        recv(("back", "x"))
        recv(("d", "pick"))
        for b in range(NB):
            rows = block(b)
            panel, inner = both(dh[0, b], dx[b]), both(back[rank_rows(0, b)], back_x[rank_rows(0, b)])
            acc[rows] += mm(inner, panel, TN)

    def last_gather():
        wait_w(4)
        for h in range(PIECES):
            recv(("ag", goes_right(h), 3, h))

        def body(i, _):
            rows = pl.ds(i * 256, 256)
            gt[rows] = (acc[rows] + mm(g[4, rows], w[4], NT)).astype(BF16)
            return 0

        lax.fori_loop(0, 3, body, 0)

    def lift():
        wait_w(0)
        wait_load("tok")
        recv(("low", "x"))
        recv(("u", "pick"))
        for b in range(NB):
            panel, inner = both(uh[0, b], ux[b]), both(low[rank_rows(0, b)], low_x[rank_rows(0, b)])
            rows = block(b)
            kv_acc[rows] = mm(tok[0, rows], w[0]) + 0.5 * mm(inner, panel, TN)

    def last_sum():
        done = 0
        for h in range(PIECES):
            recv(("rs", True, 3, h))
            recv(("rs", False, 3, h))
            for b in range(done, (h + 1) * NB // PIECES):
                rows = block(b)
                total = kv_acc[rows] + rs_right[3, rows].astype(F32) + rs_left[3, rows].astype(F32)
                kv[rows] = (live(b) * total).astype(BF16)
            done = (h + 1) * NB // PIECES

    def ag_start(h):
        ag_send(0, h, True)
        ag_send(0, h, False)

    def up_start():
        send(("u", "f0"), up_in.at[:, others], au.at[0, 0, 1], sibling)
        send("f0i", ints.at[0, 0], ints.at[0, 1], sibling)
        wait_load("u")
        f1_send("u", au, 0)

    def down_start():
        send(("d", "f0"), down_in.at[:, others], ad.at[0, 0, 1], sibling)
        wait_load("d")
        f1_send("d", ad, 0)

    def grad_rows_out():
        send("xg", g.at[0], g_sib, sibling)

    def tokens_out():
        wait_load("tok")
        send("xtok", tok.at[0], tok.at[1], sibling)

    def ints_0():
        pl.semaphore_wait(far_sem.at[0], 2)
        tell(1, 2)
        recv("f0i")
        send(("i", 1), ints.at[0], ints.at[3], q_at(1))
        send(("i", -1), ints.at[0], ints.at[1], q_at(-1))

    def ints_1():
        recv(("i", 1))
        send(("i", 2), ints.at[3], ints.at[2], q_at(1))

    def ints_2():
        recv(("i", -1))
        recv(("i", 2))
        to_smem = pltpu.make_async_copy(ints, ints_smem, copy_sem)
        to_smem.start()
        to_smem.wait()

    ag_start(2)
    ag_start(3)
    up_start()
    fetch_0("u", au)
    down_start()
    ints_0()
    rs_start(2)
    ag_start(1)
    fetch_1("u", au)
    fetch_3("u", au)
    fetch_2("u", au)
    ag_start(0)
    grad_rows_out()
    rs_start(0)
    fetch_0("d", ad)
    ints_1()
    ag_pass(0, 3)
    fetch_4("u", au)
    rs_start(1)
    rs_start(3)
    tokens_out()
    acc_first()
    rs_pass(1, 2)
    fetch_5("u", au)
    fetch_1("d", ad)
    ints_2()
    back_begin()
    ag_pass(0, 1)
    fetch_3("d", ad)
    rs_pass(1, 1)
    rs_pass(1, 0)
    fetch_2("d", ad)
    fetch_4("d", ad)
    rs_pass(1, 3)
    sum_gather("back", back_part, back_recv, back, 0.5)
    ag_pass(0, 2)
    ag_pass(0, 0)
    rs_pass(2, 2)
    fetch_5("d", ad)
    rs_pass(2, 1)
    low_begin()
    down_terms()
    ag_pass(1, 2)
    fill_table()
    ag_pass(1, 0)
    side()
    sum_gather("low", low_part, low_recv, low, 1.0)
    rs_pass(3, 2)
    rs_pass(2, 3)
    terms_pass("d", rd)
    ag_pass(1, 1)
    acc_pair(1)
    ag_pass(1, 3)
    acc_pair(2)
    up_terms()
    rs_pass(2, 0)
    ag_pass(2, 0)
    sums_send("d", rd, qd, qd_in)
    terms_pass("u", ru)
    ag_pass(2, 3)
    ag_pass(2, 2)
    rs_pass(3, 1)
    sums_pass("d", qd, qd_in)
    ag_pass(2, 1)
    acc_pair(3)
    sums_send("u", ru, qu, qu_in)
    rs_pass(3, 0)
    rs_pass(3, 3)
    sums_end("d", qd, qd_in, gd)
    sums_pass("u", qu, qu_in)
    last_gather()
    sums_end("u", qu, qu_in, gu)
    lift()
    last_sum()

    for copy in sent.values():
        copy.wait_send()


def write(gt, kv, gd, gu, gt_out, kv_out, gd_out, gu_out, sem):
    copies = []

    def copy(src, dst):
        copies.append(pltpu.make_async_copy(src, dst, sem.at[len(copies)]))
        copies[-1].start()

    for k in range(4):
        rows = pl.ds(k * (ROWS // 4), ROWS // 4)
        copy(gt.at[rows], gt_out.at[rows])
    copy(kv, kv_out)
    copy(gd, gd_out)
    copy(gu, gu_out)
    for done in copies:
        done.wait()


def local(tokens, frozen_weight, cotangent, down_maps, up_maps, stored_row, tenants, padding):
    shape = jax.ShapeDtypeStruct
    smem, anywhere = pl.BlockSpec(memory_space=pltpu.SMEM), pl.BlockSpec(memory_space=pl.ANY)
    vmem = pltpu.VMEM
    inside = pl.BlockSpec(memory_space=vmem)
    shapes = (
        shape((ROWS, COLS), BF16), shape((ROWS, FEAT), BF16),
        shape((2, RANK, FEAT), BF16), shape((2, RANK, COLS), BF16),
    )
    results = pl.pallas_call(
        kernel,
        name="projections",
        out_shape=tuple(vmem(s.shape, s.dtype) for s in shapes),
        in_specs=[smem] * 3 + [pl.BlockSpec(memory_space=pltpu.HBM)] * 5,
        out_specs=[inside] * 4,
        scratch_shapes=[
            vmem((2, ROWS, FEAT), BF16),
            vmem((NZ, FEAT, COLS), BF16),
            vmem((NZ, ROWS, COLS), BF16),
            vmem((ROWS, COLS), BF16),
            vmem((ROWS, FEAT), F32),
            vmem((ROWS, COLS), F32),
            vmem((4, ROWS, COLS), BF16),
            vmem((4, ROWS, COLS), BF16),
            vmem((2, ROWS, COLS), BF16),
            vmem((4, 4, 2, 2, HR, FEAT), BF16),
            vmem((4, 4, 2, 2, HR, COLS), BF16),
            vmem((2, NB, HR, FEAT), BF16),
            vmem((2, NB, HR, COLS), BF16),
            vmem((NB, HR, FEAT), BF16),
            vmem((NB, HR, COLS), BF16),
            vmem((4, 2, 8, 128), I32),
            pltpu.SMEM((4, 2, 8, 128), I32),
            pltpu.SMEM((16, 8), I32),
            vmem((2 * NB * HR, BR), BF16),
            vmem((NZ, 48, BR), BF16),
            vmem((2 * NB * HR, BR), BF16),
            vmem((NB * HR, BR), BF16),
            vmem((2 * NB * HR, BR), BF16),
            vmem((NZ, 48, BR), BF16),
            vmem((2 * NB * HR, BR), BF16),
            vmem((NB * HR, BR), BF16),
            vmem((49, HR, FEAT), BF16),
            vmem((49, HR, COLS), BF16),
            vmem((4, 2, 2, HR, FEAT), BF16),
            vmem((4, 2, 2, HR, COLS), BF16),
            vmem((7, 2, HR, FEAT), BF16),
            vmem((7, 2, HR, COLS), BF16),
            pltpu.SemaphoreType.DMA((N_SEM,)),
            pltpu.SemaphoreType.DMA((N_SEM,)),
            pltpu.SemaphoreType.DMA((16,)),
            pltpu.SemaphoreType.DMA,
            pltpu.SemaphoreType.REGULAR((2,)),
        ],
        compiler_params=pltpu.CompilerParams(
            collective_id=0, has_side_effects=True, vmem_limit_bytes=60 * 2**20
        ),
    )(
        stored_row, tenants, padding, tokens, frozen_weight, cotangent,
        jnp.swapaxes(down_maps, 1, 2), up_maps,
    )
    kv, gt, gd, gu = results
    gt, kv, gd, gu = pl.pallas_call(
        write,
        name="write",
        out_shape=(shapes[1], shapes[0], shapes[2], shapes[3]),
        in_specs=[inside] * 4,
        out_specs=[anywhere] * 4,
        scratch_shapes=[pltpu.SemaphoreType.DMA((7,))],
        compiler_params=pltpu.CompilerParams(vmem_limit_bytes=2 * 2**20),
    )(gt, kv, gd, gu)
    return kv, gt, jnp.swapaxes(gd, 1, 2), gu


def solution(mesh):
    placed = (
        P("dp", "tensor"),
        P("tensor", None),
        P("dp", "tensor"),
        P("dp", "tensor", None),
        P("dp", None, "tensor"),
        P(),
        P("dp"),
        P("dp"),
    )
    return jax.shard_map(
        local,
        mesh=mesh,
        in_specs=placed,
        out_specs=(
            P("dp", "tensor"),
            P("dp", "tensor"),
            P("dp", "tensor", None),
            P("dp", None, "tensor"),
        ),
        check_vma=False,
    )
```

```python
import jax
import jax.numpy as jnp
from jax import lax
from jax.experimental import pallas as pl
from jax.experimental.pallas import tpu as pltpu
from jax.sharding import PartitionSpec as P

MESH = pl.DeviceIdType.MESH
F32, BF16, I32 = jnp.float32, jnp.bfloat16, jnp.int32
NT = (((1,), (1,)), ((), ()))
TN = (((0,), (0,)), ((), ()))
NZ, NB, BR = 8, 6, 128
ROWS, PIECES, PIECE = 768, 4, 192
FEAT, COLS, RANK, HR = 1024, 256, 64, 32
N_SEM = 200


def mm(a, b, dims=None):
    if dims is None:
        return jnp.dot(a, b, preferred_element_type=F32)
    return lax.dot_general(a, b, dims, preferred_element_type=F32)


def kernel(
    stored, tenants, padding, tok_in, w_in, cot_in, down_in, up_in,
    kv, gt, gd, gu,
    tok, w, g, g_sib, acc, kv_acc, rs_right, rs_left, rs_first,
    ad, au, dh, uh, dx, ux, ints, ints_smem, table,
    low_part, low_recv, low, low_x, back_part, back_recv, back, back_x,
    rd, ru, qd, qu, qd_in, qu_in,
    send_sem, recv_sem, load_sem, copy_sem, far_sem,
):
    dp, z = lax.axis_index("dp"), lax.axis_index("tensor")
    y, x, c = dp // 8, (dp // 2) % 4, dp % 2
    mp, mq = (1 - c) * x + c * y, (1 - c) * y + c * x

    def z_at(step):
        return (dp, (z + step + NZ) % NZ)

    def chip_at(dy, dx_, core):
        return (((y + dy + 4) % 4) * 8 + ((x + dx_ + 4) % 4) * 2 + core, z)

    def p_at(step):
        return chip_at(c * step, (1 - c) * step, c)

    def q_at(step):
        return chip_at((1 - c) * step, c * step, c)

    def p_cross(step):
        return chip_at(c * step, (1 - c) * step, 1 - c)

    def q_cross(step):
        return chip_at((1 - c) * step, c * step, 1 - c)

    sibling = (dp + 1 - 2 * c, z)
    sent = {}

    def send(key, src, dst, device):
        n = len(sent)
        copy = pltpu.make_async_remote_copy(
            src_ref=src, dst_ref=dst, send_sem=send_sem.at[n], recv_sem=recv_sem.at[n],
            device_id=device, device_id_type=MESH,
        )
        copy.start()
        sent[key] = copy

    arrived, settled = set(), set()

    def settle(keys):
        for key in keys:
            if key not in settled:
                settled.add(key)
                sent[key].wait_send()

    def recv(key):
        if key not in arrived:
            arrived.add(key)
            sent[key].wait_recv()

    barrier = pltpu.get_barrier_semaphore()
    friends = [z_at(1), z_at(-1)] + [p_at(1), p_at(-1), q_at(1), q_at(-1), sibling]
    friends += [q_cross(1), q_cross(-1)]
    for friend in friends:
        pl.semaphore_signal(barrier, inc=1, device_id=friend, device_id_type=MESH)

    loads = {}

    def load(key, src, dst):
        loads[key] = pltpu.make_async_copy(src, dst, load_sem.at[len(loads)])
        loads[key].start()

    loaded = set()

    def wait_load(key):
        if key not in loaded:
            loaded.add(key)
            loads[key].wait()

    def wait_w(k):
        wait_load(("w", k))

    mine, others = pl.ds(c * HR, HR), pl.ds((1 - c) * HR, HR)
    load("g", cot_in, g.at[0])
    load("u", up_in.at[:, mine], au.at[0, 0, 0])
    load("d", down_in.at[:, mine], ad.at[0, 0, 0])
    load("tok", tok_in, tok.at[0])
    for k in (4, 3, 5, 0, 2, 6, 1, 7):
        load(("w", k), w_in.at[:, pl.ds(((z + k) % NZ) * COLS, COLS)], w.at[k])

    lane = lax.broadcasted_iota(I32, (8, 128), 1)
    tile = jnp.zeros((8, 128), I32)
    for b in range(NB):
        tile = jnp.where(lane == b, stored[tenants[b]], tile)
    ints[0, 0] = tile

    position = lax.broadcasted_iota(I32, (BR, 1), 0)

    def live(b):
        return (position < BR - padding[b]).astype(F32)

    wait_load("g")
    for b in range(NB):
        rows = pl.ds(b * BR, BR)
        g[0, rows] = (g[0, rows].astype(F32) * live(b)).astype(BF16)

    pl.semaphore_wait(barrier, len(friends))

    def tell(k, step):
        for way in (step, -step):
            pl.semaphore_signal(far_sem.at[k], inc=1, device_id=z_at(way), device_id_type=MESH)

    tell(0, 1)

    half = [pl.ds(h * PIECE, PIECE) for h in range(PIECES)]

    def goes_right(h):
        return h < PIECES // 2

    def gathers_right(h):
        return h < PIECES // 2 - 1

    def ag_send(step, h, right):
        src, dst = ((-step) % NZ, (-step - 1) % NZ) if right else (step, step + 1)
        send(("ag", right, step, h), g.at[src, half[h]], g.at[dst, half[h]], z_at(1 if right else -1))

    def ag_pass(step, h):
        for right in (True, False):
            recv(("ag", right, step, h))
            if step < 2 or gathers_right(h) == right:
                ag_send(step + 1, h, right)

    def partial(k, h):
        return mm(tok[0, half[h]], w[k])

    def rs_start(h):
        wait_load("tok")
        for right in (True, False):
            step = 0 if goes_right(h) == right else 1
            k = (4 - step) if right else (4 + step)
            wait_w(k)
            slot = 0 if right else 1
            rs_first[slot, half[h]] = partial(k, h).astype(BF16)
            dst = rs_right if right else rs_left
            send(("rs", right, step, h), rs_first.at[slot, half[h]], dst.at[step, half[h]], z_at(1 if right else -1))

    def rs_pass(step, h):
        wait_w(4 - step)
        wait_w(4 + step)
        for right in (True, False):
            if step == 1 and goes_right(h) != right:
                continue
            k = (4 - step) if right else (4 + step)
            buf = rs_right if right else rs_left
            own = partial(k, h)
            recv(("rs", right, step - 1, h))
            buf[step - 1, half[h]] = (buf[step - 1, half[h]].astype(F32) + own).astype(BF16)
            send(("rs", right, step, h), buf.at[step - 1, half[h]], buf.at[step, half[h]], z_at(1 if right else -1))

    def f1_send(name, a, r):
        send((name, "f1", 1, r), a.at[0, 0, r], a.at[0, 3, r], p_at(1))
        send((name, "f1", -1, r), a.at[0, 0, r], a.at[0, 1, r], p_at(-1))

    def f1_pass(name, a):
        recv((name, "f1", 1, 0))
        send((name, "f1x", 1), a.at[0, 3, 0], a.at[0, 2, 0], p_at(1))
        recv((name, "f1", -1, 1))
        send((name, "f1x", -1), a.at[0, 1, 1], a.at[0, 2, 1], p_at(-1))
        recv((name, "f1", 1, 1))
        recv((name, "f1", -1, 0))

    def f1_end(name):
        recv((name, "f1x", 1))
        recv((name, "f1x", -1))

    def f2_send(name, a, rp):
        send((name, "f2", 1, rp), a.at[0, rp], a.at[3, rp], q_at(1))
        send((name, "f2", -1, rp), a.at[0, rp], a.at[1, rp], q_at(-1))

    def f2_pass(name, a, rp):
        recv((name, "f2", 1, rp))
        send((name, "f2x", 1, rp), a.at[3, rp, 0], a.at[2, rp, 0], q_at(1))
        recv((name, "f2", -1, rp))
        send((name, "f2x", -1, rp), a.at[1, rp, 1], a.at[2, rp, 1], q_at(-1))

    def f2_end(name):
        for rp in range(4):
            recv((name, "f2x", 1, rp))
            recv((name, "f2x", -1, rp))

    def fetch_0(name, a):
        recv((name, "f0"))
        f1_send(name, a, 1)
        f2_send(name, a, 0)

    def fetch_1(name, a):
        f1_pass(name, a)
        f2_send(name, a, 3)
        f2_send(name, a, 1)

    def fetch_2(name, a):
        f1_end(name)
        f2_send(name, a, 2)

    def fetch_3(name, a):
        f2_pass(name, a, 0)

    def fetch_4(name, a):
        f2_pass(name, a, 3)
        f2_pass(name, a, 1)

    def fetch_5(name, a):
        f2_pass(name, a, 2)

    def place(slot):
        chip, inner = slot // 4, slot % 4
        cy, cx = chip // 4, chip % 4
        rq = ((1 - c) * cy + c * cx - mq + 4) % 4
        rp = ((1 - c) * cx + c * cy - mp + 4) % 4
        return rq, rp, (inner // 2 + c) % 2, inner % 2

    def pick(name, a, picked, out):
        f2_end(name)
        for r in (1, 0):
            for b in range(NB):
                rq, rp, core, inner = place(ints_smem[0, r, 0, b])
                picked[r, b] = a[rq, rp, core, inner]
        send((name, "pick"), picked.at[1], out, sibling)

    def sum_scatter(name, part, got):
        for k in range(1, NZ):
            rows = pl.ds(((z + k) % NZ) * 48, 48)
            send((name, "s", k), part.at[rows], got.at[k], z_at(k))

    def sum_gather(name, part, got, total, scale):
        own = pl.ds(z * 48, 48)
        value = part[own].astype(F32)
        for k in range(1, NZ):
            recv((name, "s", k))
            value = value + got[k].astype(F32)
        total[own] = (value * scale).astype(BF16)
        for k in range(1, NZ):
            send((name, "g", k), total.at[own], total.at[own], z_at(k))

    def sum_end(name, total, out):
        for k in range(1, NZ):
            recv((name, "g", k))
        send((name, "x"), total.at[pl.ds(NB * HR, NB * HR)], out, sibling)

    def rank_rows(r, b):
        return pl.ds((r * NB + b) * HR, HR)

    def block(b):
        return pl.ds(b * BR, BR)

    def back_begin():
        pick("u", au, uh, ux)
        pl.semaphore_wait(far_sem.at[1], 2)
        recv("xg")
        for b in range(NB):
            back_part[rank_rows(0, b)] = mm(uh[0, b], g[0, block(b)], NT).astype(BF16)
            back_part[rank_rows(1, b)] = mm(uh[1, b], g_sib[block(b)], NT).astype(BF16)
        sum_scatter("back", back_part, back_recv)

    def low_begin():
        pick("d", ad, dh, dx)
        recv("xtok")
        for r in (0, 1):
            for b in range(NB):
                low_part[rank_rows(r, b)] = mm(dh[r, b], tok[r, block(b)], NT).astype(BF16)
        sum_scatter("low", low_part, low_recv)

    def terms_send(name, r, core):
        src = r.at[pl.ds(core * NB, NB)]
        send((name, "t1", 1, core), src, r.at[pl.ds(36 + core * NB, NB)], q_at(1))
        send((name, "t1", -1, core), src, r.at[pl.ds(12 + core * NB, NB)], q_at(-1))

    def down_terms():
        sum_end("back", back, back_x)
        recv("xtok")
        for r in (0, 1):
            for b in range(NB):
                rd[r * NB + b] = mm(back[rank_rows(r, b)], tok[r, block(b)]).astype(BF16)
            terms_send("d", rd, r)

    def up_terms():
        sum_end("low", low, low_x)
        for b in range(NB):
            ru[b] = (0.5 * mm(low[rank_rows(0, b)], g[0, block(b)])).astype(BF16)
        terms_send("u", ru, 0)
        for b in range(NB):
            ru[NB + b] = (0.5 * mm(low[rank_rows(1, b)], g_sib[block(b)])).astype(BF16)
        terms_send("u", ru, 1)

    def terms_pass(name, r):
        recv((name, "t1", 1, 0))
        send((name, "t2", 1), r.at[pl.ds(36, NB)], r.at[pl.ds(24, NB)], q_at(1))
        recv((name, "t1", -1, 1))
        send((name, "t2", -1), r.at[pl.ds(12 + NB, NB)], r.at[pl.ds(24 + NB, NB)], q_at(-1))
        recv((name, "t1", 1, 1))
        recv((name, "t1", -1, 0))

    def fill_table():
        rd[48] = jnp.zeros((HR, FEAT), BF16)
        ru[48] = jnp.zeros((HR, COLS), BF16)

        def body(j, _):
            pj, core = (mp + j // 4) % 4, (j // 2 + c) % 2
            slot = (((1 - c) * mq + c * pj) * 4 + (1 - c) * pj + c * mq) * 4 + core * 2 + j % 2
            for i in range(4):
                for r in range(2):
                    entry = I32(48)
                    for b in range(NB):
                        entry = jnp.where(ints_smem[i, r, 0, b] == slot, (i * 2 + r) * NB + b, entry)
                    table[j, i * 2 + r] = entry
            return 0

        lax.fori_loop(0, 16, body, 0)

    def add_up(r, q, j):
        def body(inner, _):
            total = r[table[j * 4 + inner, 0]].astype(F32)
            for d in range(1, 8):
                total = total + r[table[j * 4 + inner, d]].astype(F32)
            q[j, inner // 2, inner % 2] = total.astype(BF16)
            return 0

        lax.fori_loop(0, 4, body, 0)

    def sums_send(name, r, q, q_in):
        recv((name, "t2", 1))
        recv((name, "t2", -1))
        add_up(r, q, 2)
        send((name, "q0", 1), q.at[2, 0], q_in.at[5], p_at(1))
        send((name, "q0", -1), q.at[2, 1], q_in.at[6], p_at(-1))
        add_up(r, q, 1)
        send((name, "q2", 1), q.at[1, 1], q_in.at[2], p_cross(1))
        add_up(r, q, 3)
        send((name, "q1", -1), q.at[3, 0], q_in.at[1], p_at(-1))
        add_up(r, q, 0)
        send((name, "q3"), q.at[0, 1], q_in.at[4], sibling)

    def sums_pass(name, q, q_in):
        recv((name, "q0", 1))
        q[1, 0] = (q[1, 0].astype(F32) + q_in[5].astype(F32)).astype(BF16)
        send((name, "q1", 1), q.at[1, 0], q_in.at[0], p_at(1))
        recv((name, "q0", -1))
        q[3, 1] = (q[3, 1].astype(F32) + q_in[6].astype(F32)).astype(BF16)
        send((name, "q2", -1), q.at[3, 1], q_in.at[3], p_cross(-1))

    def sums_end(name, q, q_in, out):
        recv((name, "q1", 1))
        recv((name, "q1", -1))
        recv((name, "q2", 1))
        recv((name, "q2", -1))
        recv((name, "q3"))
        for k in range(2):
            out[k, mine] = (q[0, 0, k].astype(F32) + q_in[0, k].astype(F32) + q_in[1, k].astype(F32)).astype(BF16)
            out[k, others] = (
                q_in[2, k].astype(F32) + q_in[3, k].astype(F32) + q_in[4, k].astype(F32)
            ).astype(BF16)

    def acc_first():
        wait_w(0)

        def body(i, _):
            rows = pl.ds(i * 256, 256)
            acc[rows] = mm(g[0, rows], w[0], NT)
            return 0

        lax.fori_loop(0, 3, body, 0)

    def acc_pair(k):
        wait_w(k)
        wait_w(NZ - k)

        def body(i, _):
            rows = pl.ds(i * 256, 256)
            acc[rows] += mm(g[k, rows], w[k], NT) + mm(g[NZ - k, rows], w[NZ - k], NT)
            return 0

        lax.fori_loop(0, 3, body, 0)

    def both(a, b):
        return jnp.concatenate([a, b], axis=0)

    def side():
        recv(("back", "x"))
        recv(("d", "pick"))
        for b in range(NB):
            rows = block(b)
            panel, inner = both(dh[0, b], dx[b]), both(back[rank_rows(0, b)], back_x[rank_rows(0, b)])
            acc[rows] += mm(inner, panel, TN)

    def last_gather():
        wait_w(4)
        for h in range(PIECES):
            recv(("ag", gathers_right(h), 3, h))

        def body(i, _):
            rows = pl.ds(i * 256, 256)
            gt[rows] = (acc[rows] + mm(g[4, rows], w[4], NT)).astype(BF16)
            return 0

        lax.fori_loop(0, 3, body, 0)

    def lift():
        wait_w(0)
        wait_load("tok")
        recv(("low", "x"))
        recv(("u", "pick"))
        for b in range(NB):
            panel, inner = both(uh[0, b], ux[b]), both(low[rank_rows(0, b)], low_x[rank_rows(0, b)])
            rows = block(b)
            kv_acc[rows] = mm(tok[0, rows], w[0]) + 0.5 * mm(inner, panel, TN)

    def last_sum():
        done = 0
        for h in range(PIECES):
            recv(("rs", True, 3, h))
            recv(("rs", False, 3, h))
            for b in range(done, (h + 1) * NB // PIECES):
                rows = block(b)
                total = kv_acc[rows] + rs_right[3, rows].astype(F32) + rs_left[3, rows].astype(F32)
                kv[rows] = (live(b) * total).astype(BF16)
            done = (h + 1) * NB // PIECES

    def ag_start(h):
        ag_send(0, h, True)
        ag_send(0, h, False)

    def up_start():
        send(("u", "f0"), up_in.at[:, others], au.at[0, 0, 1], sibling)
        send("f0i", ints.at[0, 0], ints.at[0, 1], sibling)
        wait_load("u")
        f1_send("u", au, 0)

    def down_start():
        send(("d", "f0"), down_in.at[:, others], ad.at[0, 0, 1], sibling)
        wait_load("d")
        f1_send("d", ad, 0)

    def grad_rows_out():
        send("xg", g.at[0], g_sib, sibling)

    def tokens_out():
        wait_load("tok")
        send("xtok", tok.at[0], tok.at[1], sibling)

    def ints_0():
        pl.semaphore_wait(far_sem.at[0], 2)
        tell(1, 2)
        recv("f0i")
        send(("i", 1), ints.at[0], ints.at[3], q_at(1))
        send(("i", -1), ints.at[0], ints.at[1], q_at(-1))

    def ints_1():
        recv(("i", 1))
        send(("i", 2), ints.at[3], ints.at[2], q_at(1))

    def ints_2():
        recv(("i", -1))
        recv(("i", 2))
        to_smem = pltpu.make_async_copy(ints, ints_smem, copy_sem)
        to_smem.start()
        to_smem.wait()

    ag_start(2)
    ag_start(3)
    up_start()
    fetch_0("u", au)
    down_start()
    ints_0()
    rs_start(2)
    ag_start(1)
    fetch_1("u", au)
    fetch_3("u", au)
    fetch_2("u", au)
    ag_start(0)
    grad_rows_out()
    rs_start(0)
    fetch_0("d", ad)
    ints_1()
    ag_pass(0, 3)
    fetch_4("u", au)
    rs_start(1)
    rs_start(3)
    tokens_out()
    acc_first()
    rs_pass(1, 2)
    fetch_5("u", au)
    fetch_1("d", ad)
    ints_2()
    back_begin()
    ag_pass(0, 1)
    fetch_3("d", ad)
    rs_pass(1, 1)
    rs_pass(1, 0)
    fetch_2("d", ad)
    fetch_4("d", ad)
    rs_pass(1, 3)
    fill_table()
    sum_gather("back", back_part, back_recv, back, 0.5)
    ag_pass(0, 2)
    ag_pass(0, 0)
    rs_pass(2, 2)
    first = list(sent)
    fetch_5("d", ad)
    rs_pass(2, 1)
    low_begin()
    down_terms()
    ag_pass(1, 2)
    ag_pass(1, 0)
    side()
    settle(first)
    sum_gather("low", low_part, low_recv, low, 1.0)
    rs_pass(3, 2)
    rs_pass(2, 3)
    terms_pass("d", rd)
    ag_pass(1, 1)
    acc_pair(1)
    ag_pass(1, 3)
    acc_pair(2)
    up_terms()
    rs_pass(2, 0)
    ag_pass(2, 0)
    sums_send("d", rd, qd, qd_in)
    terms_pass("u", ru)
    lift()
    ag_pass(2, 3)
    ag_pass(2, 2)
    rs_pass(3, 1)
    sums_pass("d", qd, qd_in)
    ag_pass(2, 1)
    acc_pair(3)
    sums_send("u", ru, qu, qu_in)
    rs_pass(3, 0)
    rs_pass(3, 3)
    sums_end("d", qd, qd_in, gd)
    sums_pass("u", qu, qu_in)
    last_gather()
    sums_end("u", qu, qu_in, gu)
    last_sum()

    settle(list(sent))


def write(gt, kv, gd, gu, gt_out, kv_out, gd_out, gu_out, sem):
    copies = []

    def copy(src, dst):
        copies.append(pltpu.make_async_copy(src, dst, sem.at[len(copies)]))
        copies[-1].start()

    for k in range(4):
        rows = pl.ds(k * (ROWS // 4), ROWS // 4)
        copy(gt.at[rows], gt_out.at[rows])
    copy(kv, kv_out)
    copy(gd, gd_out)
    copy(gu, gu_out)
    for done in copies:
        done.wait()


def local(tokens, frozen_weight, cotangent, down_maps, up_maps, stored_row, tenants, padding):
    shape = jax.ShapeDtypeStruct
    smem, anywhere = pl.BlockSpec(memory_space=pltpu.SMEM), pl.BlockSpec(memory_space=pl.ANY)
    vmem = pltpu.VMEM
    inside = pl.BlockSpec(memory_space=vmem)
    shapes = (
        shape((ROWS, COLS), BF16), shape((ROWS, FEAT), BF16),
        shape((2, RANK, FEAT), BF16), shape((2, RANK, COLS), BF16),
    )
    results = pl.pallas_call(
        kernel,
        name="projections",
        out_shape=tuple(vmem(s.shape, s.dtype) for s in shapes),
        in_specs=[smem] * 3 + [pl.BlockSpec(memory_space=pltpu.HBM)] * 5,
        out_specs=[inside] * 4,
        scratch_shapes=[
            vmem((2, ROWS, FEAT), BF16),
            vmem((NZ, FEAT, COLS), BF16),
            vmem((NZ, ROWS, COLS), BF16),
            vmem((ROWS, COLS), BF16),
            vmem((ROWS, FEAT), F32),
            vmem((ROWS, COLS), F32),
            vmem((4, ROWS, COLS), BF16),
            vmem((4, ROWS, COLS), BF16),
            vmem((2, ROWS, COLS), BF16),
            vmem((4, 4, 2, 2, HR, FEAT), BF16),
            vmem((4, 4, 2, 2, HR, COLS), BF16),
            vmem((2, NB, HR, FEAT), BF16),
            vmem((2, NB, HR, COLS), BF16),
            vmem((NB, HR, FEAT), BF16),
            vmem((NB, HR, COLS), BF16),
            vmem((4, 2, 8, 128), I32),
            pltpu.SMEM((4, 2, 8, 128), I32),
            pltpu.SMEM((16, 8), I32),
            vmem((2 * NB * HR, BR), BF16),
            vmem((NZ, 48, BR), BF16),
            vmem((2 * NB * HR, BR), BF16),
            vmem((NB * HR, BR), BF16),
            vmem((2 * NB * HR, BR), BF16),
            vmem((NZ, 48, BR), BF16),
            vmem((2 * NB * HR, BR), BF16),
            vmem((NB * HR, BR), BF16),
            vmem((49, HR, FEAT), BF16),
            vmem((49, HR, COLS), BF16),
            vmem((4, 2, 2, HR, FEAT), BF16),
            vmem((4, 2, 2, HR, COLS), BF16),
            vmem((7, 2, HR, FEAT), BF16),
            vmem((7, 2, HR, COLS), BF16),
            pltpu.SemaphoreType.DMA((N_SEM,)),
            pltpu.SemaphoreType.DMA((N_SEM,)),
            pltpu.SemaphoreType.DMA((16,)),
            pltpu.SemaphoreType.DMA,
            pltpu.SemaphoreType.REGULAR((2,)),
        ],
        compiler_params=pltpu.CompilerParams(
            collective_id=0, has_side_effects=True, vmem_limit_bytes=60 * 2**20
        ),
    )(
        stored_row, tenants, padding, tokens, frozen_weight, cotangent,
        jnp.swapaxes(down_maps, 1, 2), up_maps,
    )
    kv, gt, gd, gu = results
    gt, kv, gd, gu = pl.pallas_call(
        write,
        name="write",
        out_shape=(shapes[1], shapes[0], shapes[2], shapes[3]),
        in_specs=[inside] * 4,
        out_specs=[anywhere] * 4,
        scratch_shapes=[pltpu.SemaphoreType.DMA((7,))],
        compiler_params=pltpu.CompilerParams(vmem_limit_bytes=2 * 2**20),
    )(gt, kv, gd, gu)
    return kv, gt, jnp.swapaxes(gd, 1, 2), gu


def solution(mesh):
    placed = (
        P("dp", "tensor"),
        P("tensor", None),
        P("dp", "tensor"),
        P("dp", "tensor", None),
        P("dp", None, "tensor"),
        P(),
        P("dp"),
        P("dp"),
    )
    return jax.shard_map(
        local,
        mesh=mesh,
        in_specs=placed,
        out_specs=(
            P("dp", "tensor"),
            P("dp", "tensor"),
            P("dp", "tensor", None),
            P("dp", None, "tensor"),
        ),
        check_vma=False,
    )
```
